128 devices in a mesh: inner: 8 (over z_lo, y), outer: 16 (over x, z_hi, core).
Axes of the slice: x: 4, y: 4, z: 4 (z_hi: 2, z_lo: 2; z = z_hi * 2 + z_lo), core: 2. Of those that a mesh axis runs over, the one named last changes fastest.
Arguments:
- queries: bfloat16 [262144, 256], P(('outer', 'inner')), may hold values from -24 to 24
- keys: bfloat16 [262144, 256], P(('outer', 'inner')), may hold values from -24 to 24
- values: bfloat16 [262144, 256], P(('outer', 'inner')), may hold values from -6 to 6
- offsets_group: int32 [16, 2], replicated, may hold values from 0 to 7
- offsets_global: int32 [2], replicated, may hold values from 0 to 127
- out_weight: bfloat16 [256, 4096], replicated, may hold values from -0.375 to 0.375
Outputs:
- projected: bfloat16 [262144, 4096], P(('outer', 'inner'))
The draws below stay inside these ranges and needn't reach their ends.
All inputs are finite; a program needn't handle non-finite values.
Results may differ from the reference program's by a relative error of at most 0.0054.
Values may be sent and summed in bfloat16 or wider, within the bound.
A program may use at most 128 MiB of HBM per device.

```python
import jax
import jax.numpy as jnp
from jax import lax

D = 4096
HD = 128
HEADS = 2
TOK_DEV = 2048
TOKENS = 262144
SEG1 = 16384
R1 = 8
R2 = 128


def draw_queries(key, part):
    key = jax.random.fold_in(key, 11)
    noise = jnp.clip(jax.random.normal(key, (TOKENS, HEADS * HD), jnp.float32), -4.0, 4.0)
    return noise.astype(jnp.bfloat16)


def draw_keys(key, part):
    key = jax.random.fold_in(key, 23)
    noise = jnp.clip(jax.random.normal(key, (TOKENS, HEADS * HD), jnp.float32), -4.0, 4.0)
    return noise.astype(jnp.bfloat16)


def with_ends(result, rng, least, high):
    longest = result.shape.index(max(result.shape))
    spots = []
    for shift in (0, 1):
        where = [jax.random.randint(jax.random.fold_in(rng, axis), (), 0, length) for axis, length in enumerate(result.shape)]
        where[longest] = (where[longest] + shift) % result.shape[longest]
        spots.append(tuple(where))
    return result.at[spots[0]].set(least).at[spots[1]].set(high)


def block_scale(stream_key, dims, shards, low, largest):
    def one(position, parts):
        steps = jax.random.uniform(jax.random.fold_in(jax.random.fold_in(stream_key, 6), position), (parts,), jnp.float32, low / len(shards), largest / len(shards))
        return jnp.repeat(jnp.exp(steps), dims[position] // parts).reshape((-1,) + (1,) * (len(dims) - position - 1))

    level = one(*shards[0])
    for cut in shards[1:]:
        level = level * one(*cut)
    return level


def normal_values(key, dims, width, bound, cuts=(), kind=jnp.bfloat16):
    values = jax.random.normal(key, dims, jnp.float32) * width
    if len(cuts) > 0:
        values = block_scale(key, dims, cuts, -0.22, 0.18) * values
    return jnp.clip(values, min=-bound, max=bound).astype(kind)


def setup_inputs(seed: int = 0) -> dict:
    splits = jax.random.split(jax.random.key(seed), 7)
    return {
        "queries": draw_queries(jax.random.fold_in(splits[6], 71), 0),
        "keys": draw_keys(jax.random.fold_in(splits[6], 71), 0),
        "values": normal_values(splits[2], (TOKENS, HEADS * HD), 1.0, 6.0, ((0, 128),)),
        "offsets_group": with_ends(jax.random.randint(splits[3], (TOKENS // SEG1, HEADS), 0, R1), jax.random.fold_in(splits[3], 1), 0, R1 - 1).astype(jnp.int32),
        "offsets_global": jax.random.randint(splits[4], (HEADS,), 0, R2).astype(jnp.int32),
        "out_weight": normal_values(splits[5], (HEADS * HD, D), (HEADS * HD) ** -0.5, 0.375),
    }


def attend(query, keys_in, values_in, query_pos, key_pos):
    scores = jnp.dot(query, keys_in.T, preferred_element_type=jnp.float32) * (HD ** -0.5)
    scores = jnp.where(key_pos[None, :] <= query_pos[:, None], scores, -jnp.inf)
    top = jnp.max(scores, axis=1)
    expo = jnp.exp(scores - top[:, None])
    denom = jnp.sum(expo, axis=1)
    out = jnp.dot(expo.astype(jnp.bfloat16), values_in, preferred_element_type=jnp.float32) / denom[:, None]
    return out, top + jnp.log(denom)


def pick_rows(part, offset, rate):
    rows = part.shape[0]
    return lax.dynamic_index_in_dim(part.reshape(rows // rate, rate, part.shape[1]), offset, 1, False)


def select_rows(matrix, head, offset, rate):
    return pick_rows(matrix[:, head * HD:(head + 1) * HD], offset, rate)


def blend(acc, lse, out_p, lse_p, offset, rate):
    rows = acc.shape[0]
    acc3 = acc.reshape(rows // rate, rate, HD)
    lse2 = lse.reshape(rows // rate, rate)
    prior = lax.dynamic_index_in_dim(acc3, offset, 1, False)
    prior_lse = lax.dynamic_index_in_dim(lse2, offset, 1, False)
    fresh = jnp.logaddexp(prior_lse, lse_p)
    mixed = prior * jnp.exp(prior_lse - fresh)[:, None] + out_p * jnp.exp(lse_p - fresh)[:, None]
    acc3 = lax.dynamic_update_index_in_dim(acc3, mixed, offset, 1)
    lse2 = lax.dynamic_update_index_in_dim(lse2, fresh, offset, 1)
    return acc3.reshape(rows, HD), lse2.reshape(rows)


def segmented(q_rows, k_rows, v_rows, seg_len):
    count = q_rows.shape[0] // seg_len
    spots = jnp.arange(seg_len, dtype=jnp.int32)

    def one_segment(triple):
        return attend(triple[0], triple[1], triple[2], spots, spots)

    out, lse = lax.map(one_segment, (q_rows.reshape(count, seg_len, HD), k_rows.reshape(count, seg_len, HD), v_rows.reshape(count, seg_len, HD)))
    return out.reshape(count * seg_len, HD), lse.reshape(count * seg_len)


def group_pattern(q_head, k_head, v_head, acc, lse, offs):
    count = TOKENS // SEG1
    spots = jnp.arange(SEG1 // R1, dtype=jnp.int32)

    def one_segment(item):
        q_seg, k_seg, v_seg, a_seg, l_seg, offset = item
        out_p, lse_p = attend(pick_rows(q_seg, offset, R1), pick_rows(k_seg, offset, R1), pick_rows(v_seg, offset, R1), spots, spots)
        return blend(a_seg, l_seg, out_p, lse_p, offset, R1)

    acc_new, lse_new = lax.map(one_segment, (q_head.reshape(count, SEG1, HD), k_head.reshape(count, SEG1, HD), v_head.reshape(count, SEG1, HD), acc.reshape(count, SEG1, HD), lse.reshape(count, SEG1), offs))
    return acc_new.reshape(TOKENS, HD), lse_new.reshape(TOKENS)


def reference(queries, keys, values, offsets_group, offsets_global, out_weight):
    heads_out = []
    for head in range(HEADS):
        cols = slice(head * HD, (head + 1) * HD)
        acc, lse = segmented(queries[:, cols], keys[:, cols], values[:, cols], TOK_DEV)
        acc, lse = group_pattern(queries[:, cols], keys[:, cols], values[:, cols], acc, lse, offsets_group[:, head])
        offset = offsets_global[head]
        out_p, lse_p = segmented(select_rows(queries, head, offset, R2), select_rows(keys, head, offset, R2), select_rows(values, head, offset, R2), TOKENS // R2)
        acc, lse = blend(acc, lse, out_p, lse_p, offset, R2)
        heads_out.append(acc)
    attended = jnp.concatenate(heads_out, axis=1).astype(jnp.bfloat16)
    return jnp.dot(attended, out_weight, preferred_element_type=jnp.float32).astype(jnp.bfloat16)
```

```python
import functools

import jax
import jax.numpy as jnp
from jax import lax
from jax.experimental import pallas as pl
from jax.experimental.pallas import tpu as pltpu
from jax.sharding import PartitionSpec as P

HD = 128
HEADS = 2
ROWS = 2048
RING = 4
PLANES = 2
GROUP = RING * PLANES
GROUPS = 16
SEL = ROWS // GROUP
WHOLE = ROWS // (GROUP * GROUPS)
BQ = 256
BLOCKS = ROWS // BQ
SCALE = HD**-0.5 * 1.4426950408889634
NEG = -1e30
F32 = jnp.float32
BF16 = jnp.bfloat16


def iota(shape, dim):
    return lax.broadcasted_iota(jnp.int32, shape, dim)


def cols(head):
    return slice(head * HD, (head + 1) * HD)


def dot_t(a, b):
    return lax.dot_general(a, b, (((1,), (1,)), ((), ())), preferred_element_type=F32)


def dot(a, b):
    return jnp.dot(a, b, preferred_element_type=F32)


def wide(column, rows):
    return jnp.broadcast_to(column, (rows, HD))


def finish(scores, values):
    rows = scores.shape[0]
    top = jnp.max(scores, axis=1, keepdims=True)
    expo = jnp.exp2((scores - top) * SCALE)
    total = jnp.sum(expo, axis=1, keepdims=True)
    out = dot(expo.astype(BF16), values) / total
    return out, wide(top * SCALE + jnp.log2(total), rows)


def local_tile(q_ref, k_ref, vx_ref, block, head):
    low = block * BQ
    high = low + BQ
    scores = dot_t(q_ref[low:high, cols(head)], k_ref[0:high, cols(head)])
    diag = jnp.where(iota((BQ, BQ), 1) <= iota((BQ, BQ), 0), scores[:, low:], NEG)
    scores = diag if block == 0 else jnp.concatenate([scores[:, :low], diag], axis=1)
    top = jnp.max(scores, axis=1, keepdims=True)
    expo = jnp.exp2((scores - top) * SCALE)
    out = dot(expo.astype(BF16), vx_ref[0:high, head * 2 * HD : (head + 1) * 2 * HD])
    total = out[:, HD:]
    return out[:, :HD] / total, top * SCALE + jnp.log2(total)


def merge(out0, lse0, out1, lse1, out2, lse2, offset1, offset2):
    spots = iota((BQ, HD), 0)
    n1 = BQ // GROUP
    n2 = BQ // (GROUP * GROUPS)

    def spread(part, count):
        return jnp.broadcast_to(part[:, None, :], (count, BQ // count, HD)).reshape(BQ, HD)

    e1 = jnp.where(lax.rem(spots, GROUP) == offset1, spread(lse1, n1), NEG)
    e2 = jnp.where(lax.rem(spots, GROUP * GROUPS) == offset2, spread(lse2, n2), NEG)
    top = jnp.maximum(jnp.maximum(lse0, e1), e2)
    w0 = jnp.exp2(lse0 - top)
    w1 = jnp.exp2(e1 - top)
    w2 = jnp.exp2(e2 - top)
    mixed = w0 * out0 + w1 * spread(out1, n1) + w2 * spread(out2, n2)
    return (mixed / (w0 + w1 + w2)).astype(BF16)


def attention_kernel(
    offg_ref, offw_ref, q_ref, k_ref, v_ref, att_ref,
    vx, out0, lse0, out1, lse1, out2, lse2,
    gk, gv, gq, gqp, gop, gor, gsp, gsr,
    nkv, nq, no_out, no_in,
    send, recv, wq_send, wq_recv, wo_send, wo_recv,
):
    outer = lax.axis_index("outer")
    inner = lax.axis_index("inner")
    plane = inner // RING
    y = inner % RING
    left_y = (y + RING - 1) % RING
    right_y = (y + 1) % RING
    left = plane * RING + left_y
    right = plane * RING + right_y
    across = (1 - plane) * RING + y

    barrier = pltpu.get_barrier_semaphore()
    for peer in (left, right, across):
        pl.semaphore_signal(barrier, inc=1, device_id={"inner": peer}, device_id_type=pl.DeviceIdType.MESH)

    def greet(step, carry):
        pl.semaphore_signal(
            barrier, inc=1, device_id={"outer": (outer + step) % GROUPS}, device_id_type=pl.DeviceIdType.MESH
        )
        return carry

    lax.fori_loop(1, GROUPS, greet, 0)

    def remote(src, dst, index, axis, peer):
        return pltpu.make_async_remote_copy(
            src_ref=src, dst_ref=dst, send_sem=send.at[index], recv_sem=recv.at[index],
            device_id={axis: peer}, device_id_type=pl.DeviceIdType.MESH,
        )

    offs1 = [offg_ref[outer, head] for head in range(HEADS)]
    offs2 = [offw_ref[head] for head in range(HEADS)]
    n1 = BQ // GROUP
    pick1 = [
        (iota((n1, BQ), 1) == iota((n1, BQ), 0) * GROUP + offs1[head]).astype(F32).astype(BF16)
        for head in range(HEADS)
    ]
    own1 = pl.multiple_of(y * SEL, SEL)
    own2 = pl.multiple_of(inner * WHOLE, WHOLE)
    whole = [[jnp.zeros((WHOLE, HD), F32) for _ in range(HEADS)] for _ in range(3)]
    for block in range(BLOCKS):
        low = block * BQ
        pick2 = [
            (iota((WHOLE, BQ), 1) + low == iota((WHOLE, BQ), 0) * (GROUP * GROUPS) + offs2[head])
            .astype(F32).astype(BF16)
            for head in range(HEADS)
        ]
        pick = jnp.concatenate(pick1 + pick2, axis=0)
        for index, ref in enumerate((k_ref, v_ref, q_ref)):
            got = dot(pick, ref[low : low + BQ, :])
            for head in range(HEADS):
                rows1 = got[head * n1 : (head + 1) * n1, cols(head)].astype(BF16)
                if index == 2:
                    gq[head, block * n1 : (block + 1) * n1, :] = rows1
                else:
                    (gk, gv)[index][head, pl.ds(own1 + block * n1, n1), :] = rows1
                base = HEADS * n1 + head * WHOLE
                whole[index][head] += got[base : base + WHOLE, cols(head)]
    for head in range(HEADS):
        nkv[pl.ds(own2, WHOLE), cols(head)] = whole[0][head].astype(BF16)
        nkv[pl.ds(own2, WHOLE), cols(HEADS + head)] = whole[1][head].astype(BF16)
        nq[pl.ds(pl.multiple_of(outer * WHOLE, WHOLE), WHOLE), cols(head)] = whole[2][head].astype(BF16)

    pl.semaphore_wait(barrier, 3 + GROUPS - 1)

    def whole_slot(index):
        return pl.ds(pl.multiple_of(index * WHOLE, WHOLE), WHOLE)

    mine = nkv.at[whole_slot(inner)]
    nkv_right = remote(mine, mine, 0, "inner", right)
    nkv_left = remote(mine, mine, 1, "inner", left)
    from_left = nkv.at[whole_slot(left), 0 : HEADS * HD]
    from_right = nkv.at[whole_slot(right), HEADS * HD : 2 * HEADS * HD]
    nkv_relay_right = remote(from_left, from_left, 2, "inner", right)
    nkv_relay_left = remote(from_right, from_right, 3, "inner", left)
    half = pl.ds(pl.multiple_of(plane * RING * WHOLE, RING * WHOLE), RING * WHOLE)
    nkv_across = remote(nkv.at[half], nkv.at[half], 4, "inner", across)

    def query_copy(peer, slot):
        rows = whole_slot(slot)
        return pltpu.make_async_remote_copy(
            src_ref=nq.at[whole_slot(outer)], dst_ref=nq.at[rows],
            send_sem=wq_send.at[peer], recv_sem=wq_recv.at[slot],
            device_id={"outer": peer}, device_id_type=pl.DeviceIdType.MESH,
        )

    def result_copy(peer, slot):
        return pltpu.make_async_remote_copy(
            src_ref=no_out.at[whole_slot(peer)], dst_ref=no_in.at[whole_slot(slot)],
            send_sem=wo_send.at[peer], recv_sem=wo_recv.at[slot],
            device_id={"outer": peer}, device_id_type=pl.DeviceIdType.MESH,
        )

    def each_peer(act):
        def body(step, carry):
            act((outer + step) % GROUPS)
            return carry

        lax.fori_loop(1, GROUPS, body, 0)

    def ring_copy(buffer, head, slot_y, index, peer):
        part = buffer.at[head, pl.ds(pl.multiple_of(slot_y * SEL, SEL), SEL)]
        return remote(part, part, index, "inner", peer)

    ring = []
    for head in range(HEADS):
        base = 5 + head * 9
        ring.append(
            dict(
                k_right=ring_copy(gk, head, y, base, right),
                v_right=ring_copy(gv, head, y, base + 1, right),
                v_left=ring_copy(gv, head, y, base + 2, left),
                k_left=ring_copy(gk, head, y, base + 3, left),
                relay_right=ring_copy(gk, head, left_y, base + 4, right),
                relay_left=ring_copy(gv, head, right_y, base + 5, left),
                q=remote(gq.at[head], gqp.at[head], base + 6, "inner", across),
                o=remote(gop.at[head], gor.at[head], base + 7, "inner", across),
                s=remote(gsp.at[head], gsr.at[head], base + 8, "inner", across),
            )
        )

    def start(*copies):
        for copy in copies:
            copy.start()

    def arrived(*copies):
        for copy in copies:
            copy.wait_recv()

    def own_sends(head):
        c = ring[head]
        start(c["k_right"], c["v_left"], c["v_right"], c["k_left"])

    start(nkv_right, nkv_left)
    own_sends(0)
    each_peer(lambda peer: query_copy(peer, outer).start())
    start(ring[0]["q"], ring[1]["q"])

    for head in range(HEADS):
        vx[:, 2 * head * HD : (2 * head + 1) * HD] = v_ref[:, cols(head)]
        vx[:, (2 * head + 1) * HD : (2 * head + 2) * HD] = jnp.ones((ROWS, HD), BF16)

    def local(block):
        for head in range(HEADS):
            out, lse = local_tile(q_ref, k_ref, vx, block, head)
            out0[block * BQ : (block + 1) * BQ, cols(head)] = out
            lse0[block * BQ : (block + 1) * BQ, cols(head)] = lse

    def group_across(head):
        out, lse = finish(dot_t(gqp[head], gk[head]), gv[head])
        gop[head] = out.astype(BF16)
        gsp[head] = lse.T[0:8, :]
        start(ring[head]["o"], ring[head]["s"])

    def group_own(head):
        scores = dot_t(gq[head], gk[head])
        shape = (SEL, RING * SEL)
        out, lse = finish(jnp.where(iota(shape, 1) <= iota(shape, 0) + y * SEL, scores, NEG), gv[head])
        out1[:, cols(head)] = out
        lse1[:, cols(head)] = lse

    def whole_all():
        rows = GROUPS * WHOLE
        keys = GROUP * WHOLE
        shape = (rows, keys)
        row = iota(shape, 0)
        query_pos = (row // WHOLE) * keys + inner * WHOLE + row % WHOLE
        allowed = iota(shape, 1) + outer * keys <= query_pos
        lane = iota((rows, HD), 1)
        stats = jnp.zeros((rows, HD), F32)
        for head in range(HEADS):
            scores = dot_t(nq[:, cols(head)], nkv[:, cols(head)])
            out, lse = finish(jnp.where(allowed, scores, NEG), nkv[:, cols(HEADS + head)])
            no_out[:, cols(head)] = out.astype(BF16)
            for part in range(3):
                term = lse.astype(BF16).astype(F32)
                lse = lse - term
                stats = jnp.where(lane // 16 == 3 * head + part, term, stats)
        no_out[:, cols(HEADS)] = stats.astype(BF16)
        own = whole_slot(outer)
        no_in[own, :] = no_out[own, :]

    local(7)
    arrived(nkv_right, nkv_left)
    start(nkv_relay_right, nkv_relay_left)
    arrived(ring[0]["k_right"], ring[0]["v_left"])
    start(ring[0]["relay_right"], ring[0]["relay_left"])
    own_sends(1)
    local(6)
    arrived(nkv_relay_right, nkv_relay_left)
    start(nkv_across)
    local(5)
    arrived(nkv_across)
    each_peer(lambda peer: query_copy(peer, peer).wait_recv())
    whole_all()
    each_peer(lambda peer: result_copy(peer, outer).start())
    arrived(ring[0]["v_right"], ring[0]["k_left"], ring[0]["relay_right"], ring[0]["relay_left"], ring[0]["q"])
    group_across(0)
    arrived(ring[1]["k_right"], ring[1]["v_left"])
    start(ring[1]["relay_right"], ring[1]["relay_left"])
    group_own(0)
    local(4)
    local(3)
    arrived(ring[1]["v_right"], ring[1]["k_left"], ring[1]["relay_right"], ring[1]["relay_left"], ring[1]["q"])
    group_across(1)
    group_own(1)
    local(2)
    local(1)
    local(0)

    each_peer(lambda peer: result_copy(peer, peer).wait_recv())
    for head in range(HEADS):
        parts = no_in[:, cols(head)].astype(F32).reshape(GROUPS, WHOLE, HD)
        stats = no_in[:, cols(HEADS)].astype(F32)
        lane = 48 * head
        lse = stats[:, lane : lane + 1] + stats[:, lane + 16 : lane + 17] + stats[:, lane + 32 : lane + 33]
        lse = wide(lse, GROUPS * WHOLE).reshape(GROUPS, WHOLE, HD)
        top = jnp.max(lse, axis=0)
        weight = jnp.exp2(lse - top[None])
        total = jnp.sum(weight, axis=0)
        out2[:, cols(head)] = jnp.sum(weight * parts, axis=0) / total
        lse2[:, cols(head)] = top + jnp.log2(total)

    for head in range(HEADS):
        arrived(ring[head]["o"], ring[head]["s"])
        there = jnp.broadcast_to(gsr[head, 0:1, :], (HD, SEL)).T
        there = jnp.where(plane == 1, there, NEG)
        here = lse1[:, cols(head)]
        top = jnp.maximum(here, there)
        w_here = jnp.exp2(here - top)
        w_there = jnp.exp2(there - top)
        total = w_here + w_there
        out1[:, cols(head)] = (w_here * out1[:, cols(head)] + w_there * gor[head].astype(F32)) / total
        lse1[:, cols(head)] = top + jnp.log2(total)

    n2 = BQ // (GROUP * GROUPS)
    for block in range(BLOCKS):
        rows = slice(block * BQ, (block + 1) * BQ)
        rows1 = slice(block * n1, (block + 1) * n1)
        rows2 = slice(block * n2, (block + 1) * n2)
        for head in range(HEADS):
            c = cols(head)
            att_ref[rows, c] = merge(
                out0[rows, c], lse0[rows, c], out1[rows1, c], lse1[rows1, c], out2[rows2, c], lse2[rows2, c],
                offs1[head], offs2[head],
            )

    for copy in (nkv_right, nkv_left, nkv_relay_right, nkv_relay_left, nkv_across):
        copy.wait_send()
    for head in range(HEADS):
        for copy in ring[head].values():
            copy.wait_send()
    each_peer(lambda peer: query_copy(peer, outer).wait_send())
    each_peer(lambda peer: result_copy(peer, outer).wait_send())


def attention(queries, keys, values, offsets_group, offsets_global):
    vmem = pl.BlockSpec(memory_space=pltpu.VMEM)
    smem = pl.BlockSpec(memory_space=pltpu.SMEM)
    dma = pltpu.SemaphoreType.DMA
    return pl.pallas_call(
        attention_kernel,
        out_shape=jax.ShapeDtypeStruct((ROWS, HEADS * HD), BF16),
        in_specs=[smem, smem, vmem, vmem, vmem],
        out_specs=vmem,
        scratch_shapes=[
            pltpu.VMEM((ROWS, 2 * HEADS * HD), BF16),
            pltpu.VMEM((ROWS, HEADS * HD), F32),
            pltpu.VMEM((ROWS, HEADS * HD), F32),
            pltpu.VMEM((SEL, HEADS * HD), F32),
            pltpu.VMEM((SEL, HEADS * HD), F32),
            pltpu.VMEM((WHOLE, HEADS * HD), F32),
            pltpu.VMEM((WHOLE, HEADS * HD), F32),
            pltpu.VMEM((HEADS, RING * SEL, HD), BF16),
            pltpu.VMEM((HEADS, RING * SEL, HD), BF16),
            pltpu.VMEM((HEADS, SEL, HD), BF16),
            pltpu.VMEM((HEADS, SEL, HD), BF16),
            pltpu.VMEM((HEADS, SEL, HD), BF16),
            pltpu.VMEM((HEADS, SEL, HD), BF16),
            pltpu.VMEM((HEADS, 8, SEL), F32),
            pltpu.VMEM((HEADS, 8, SEL), F32),
            pltpu.VMEM((GROUP * WHOLE, 2 * HEADS * HD), BF16),
            pltpu.VMEM((GROUPS * WHOLE, HEADS * HD), BF16),
            pltpu.VMEM((GROUPS * WHOLE, (HEADS + 1) * HD), BF16),
            pltpu.VMEM((GROUPS * WHOLE, (HEADS + 1) * HD), BF16),
            dma((23,)),
            dma((23,)),
            dma((GROUPS,)),
            dma((GROUPS,)),
            dma((GROUPS,)),
            dma((GROUPS,)),
        ],
        compiler_params=pltpu.CompilerParams(
            collective_id=0, has_side_effects=True, vmem_limit_bytes=40 * 2**20
        ),
        cost_estimate=pl.CostEstimate(flops=5 * 10**9, bytes_accessed=4 * 2**20, transcendentals=6 * 10**6),
        name="attention",
    )(offsets_group, offsets_global, queries, keys, values)


CHUNK = 256
CHUNKS = ROWS // CHUNK
SLOTS = 4


def project_kernel(a_ref, w_ref, o_ref, buf, sem):
    def copy(chunk):
        return pltpu.make_async_copy(
            buf.at[chunk % SLOTS], o_ref.at[pl.ds(chunk * CHUNK, CHUNK)], sem.at[chunk % SLOTS]
        )

    for chunk in range(CHUNKS):
        if chunk >= SLOTS:
            copy(chunk - SLOTS).wait()
        buf[chunk % SLOTS] = dot(a_ref[chunk * CHUNK : (chunk + 1) * CHUNK, :], w_ref[...]).astype(BF16)
        copy(chunk).start()
    for chunk in range(CHUNKS - SLOTS, CHUNKS):
        copy(chunk).wait()


def project(attended, weight):
    vmem = pl.BlockSpec(memory_space=pltpu.VMEM)
    width = weight.shape[1]
    return pl.pallas_call(
        project_kernel,
        out_shape=jax.ShapeDtypeStruct((ROWS, width), BF16),
        in_specs=[vmem, vmem],
        out_specs=pl.BlockSpec(memory_space=pl.ANY),
        scratch_shapes=[pltpu.VMEM((SLOTS, CHUNK, width), BF16), pltpu.SemaphoreType.DMA((SLOTS,))],
        compiler_params=pltpu.CompilerParams(vmem_limit_bytes=40 * 2**20),
        cost_estimate=pl.CostEstimate(flops=43 * 10**8, bytes_accessed=19 * 2**20, transcendentals=0),
        name="project",
    )(attended, weight)


def per_device(queries, keys, values, offsets_group, offsets_global, out_weight):
    attended = attention(queries, keys, values, offsets_group, offsets_global)
    return project(attended, out_weight)


def solution(mesh):
    rows = P(("outer", "inner"), None)
    return jax.shard_map(
        per_device, mesh=mesh, in_specs=(rows, rows, rows, P(), P(), P()), out_specs=rows, check_vma=False
    )
```

```python
import functools

import jax
import jax.numpy as jnp
from jax import lax
from jax.experimental import pallas as pl
from jax.experimental.pallas import tpu as pltpu
from jax.sharding import PartitionSpec as P

HD = 128
HEADS = 2
ROWS = 2048
RING = 4
PLANES = 2
GROUP = RING * PLANES
GROUPS = 16
CORES = 2
CHIPS = GROUPS // CORES
SEL = ROWS // GROUP
WHOLE = ROWS // (GROUP * GROUPS)
BQ = 256
BLOCKS = ROWS // BQ
SCALE = HD**-0.5 * 1.4426950408889634
NEG = -1e30
F32 = jnp.float32
BF16 = jnp.bfloat16


def iota(shape, dim):
    return lax.broadcasted_iota(jnp.int32, shape, dim)


def cols(head):
    return slice(head * HD, (head + 1) * HD)


def dot_t(a, b):
    return lax.dot_general(a, b, (((1,), (1,)), ((), ())), preferred_element_type=F32)


def dot(a, b):
    return jnp.dot(a, b, preferred_element_type=F32)


def wide(column, rows):
    return jnp.broadcast_to(column, (rows, HD))


def finish(scores, values):
    rows = scores.shape[0]
    top = jnp.max(scores, axis=1, keepdims=True)
    expo = jnp.exp2((scores - top) * SCALE)
    total = jnp.sum(expo, axis=1, keepdims=True)
    out = dot(expo.astype(BF16), values) / total
    return out, wide(top * SCALE + jnp.log2(total), rows)


def local_tile(q_ref, k_ref, vx_ref, block, head):
    low = block * BQ
    high = low + BQ
    scores = dot_t(q_ref[low:high, cols(head)], k_ref[0:high, cols(head)])
    diag = jnp.where(iota((BQ, BQ), 1) <= iota((BQ, BQ), 0), scores[:, low:], NEG)
    scores = diag if block == 0 else jnp.concatenate([scores[:, :low], diag], axis=1)
    top = jnp.max(scores, axis=1, keepdims=True)
    expo = jnp.exp2((scores - top) * SCALE)
    out = dot(expo.astype(BF16), vx_ref[0:high, head * 2 * HD : (head + 1) * 2 * HD])
    total = out[:, HD:]
    return out[:, :HD] / total, top * SCALE + jnp.log2(total)


def merge(parts):
    top = parts[0][1]
    for _, lse in parts[1:]:
        top = jnp.maximum(top, lse)
    weights = [jnp.exp2(lse - top) for _, lse in parts]
    out = sum(weight * part for weight, (part, _) in zip(weights, parts))
    total = sum(weights)
    return out / total, top + jnp.log2(total)


def three_terms(value, place):
    result = jnp.zeros(value.shape, F32)
    for term in range(3):
        head = value.astype(BF16).astype(F32)
        value = value - head
        result = jnp.where(place == term, head, result)
    return result.astype(BF16)


def pack_lse(lse):
    flat = lse.T[0:16, :]
    row = iota((16, HD), 0)
    return three_terms(jnp.where(row % 2 == 0, flat[:, :HD], flat[:, HD:]), row // 2)


def unpack_lse(packed):
    rows = packed.astype(F32)
    halves = [rows[h : h + 1] + rows[h + 2 : h + 3] + rows[h + 4 : h + 5] for h in range(2)]
    flat = jnp.concatenate(halves, axis=1)
    return jnp.broadcast_to(flat, (HD, SEL)).T


def attention_kernel(
    offg_hbm, offw_hbm, q_hbm, k_hbm, v_hbm,
    att_hbm, small_hbm,
    offg_ref, offw_ref, q_ref, k_ref, v_ref, vx, att, small, out0, lse0, out1, lse1,
    gk, gv, gq, gqr, gos, gor,
    nkv, nq, no_out, no_in,
    load, store, send, recv, wk_send, wk_recv, wq_send, wq_recv, wo_send, wo_recv,
):
    outer = lax.axis_index("outer")
    inner = lax.axis_index("inner")
    plane = inner // RING
    y = inner % RING
    chip = outer // CORES
    core = outer % CORES
    base = plane * RING
    pair = base + (y // 2) * 2 + 1 - y % 2
    across = (1 - plane) * RING + y
    reverse = base + RING - 1 - y
    diagonal = (1 - plane) * RING + RING - 1 - y
    other_core = chip * CORES + 1 - core
    mesh_id = pl.DeviceIdType.MESH

    barrier = pltpu.get_barrier_semaphore()

    def greet_inner(step, carry):
        pl.semaphore_signal(barrier, inc=1, device_id={"inner": (inner + step) % GROUP}, device_id_type=mesh_id)
        return carry

    def greet_outer(peer, carry):
        pl.semaphore_signal(barrier, inc=1, device_id={"outer": peer * CORES + core}, device_id_type=mesh_id)
        return carry

    lax.fori_loop(1, GROUP, greet_inner, 0)
    lax.fori_loop(chip + 1, CHIPS, greet_outer, 0)
    pl.semaphore_signal(barrier, inc=1, device_id={"outer": other_core}, device_id_type=mesh_id)

    loads = [
        pltpu.make_async_copy(src, dst, load.at[index])
        for index, (src, dst) in enumerate(
            ((offg_hbm, offg_ref), (offw_hbm, offw_ref), (k_hbm, k_ref), (v_hbm, v_ref), (q_hbm, q_ref))
        )
    ]
    for copy in loads:
        copy.start()
    loads[0].wait()
    loads[1].wait()

    offs1 = [offg_ref[head, outer] for head in range(HEADS)]
    offs2 = [offw_ref[head] for head in range(HEADS)]
    row8 = iota((8, HD), 0)
    offsets = jnp.where(
        row8 == 0, offs1[0], jnp.where(row8 == 1, offs1[1], jnp.where(row8 == 2, offs2[0], offs2[1]))
    )
    for head in range(HEADS):
        small[SEL + WHOLE : SEL + WHOLE + 8, cols(head)] = offsets.astype(F32)
    n1 = BQ // GROUP
    pick1 = [
        (iota((n1, BQ), 1) == iota((n1, BQ), 0) * GROUP + offs1[head]).astype(F32).astype(BF16)
        for head in range(HEADS)
    ]
    picks = []
    for block in range(BLOCKS):
        pick2 = [
            (iota((WHOLE, BQ), 1) + block * BQ == iota((WHOLE, BQ), 0) * (GROUP * GROUPS) + offs2[head])
            .astype(F32).astype(BF16)
            for head in range(HEADS)
        ]
        picks.append(jnp.concatenate(pick1 + pick2, axis=0))
    own1 = pl.multiple_of((y % 2) * SEL, SEL)
    own2 = pl.multiple_of(inner * WHOLE, WHOLE)
    own3 = pl.multiple_of(chip * WHOLE, WHOLE)
    def select(index):
        ref = (k_ref, v_ref, q_ref)[index]
        loads[2 + index].wait()
        whole = [jnp.zeros((WHOLE, HD), F32) for _ in range(HEADS)]
        for block in range(BLOCKS):
            got = dot(picks[block], ref[block * BQ : (block + 1) * BQ, :])
            for head in range(HEADS):
                rows1 = got[head * n1 : (head + 1) * n1, cols(head)].astype(BF16)
                if index == 2:
                    gq[head, block * n1 : (block + 1) * n1, :] = rows1
                else:
                    (gk, gv)[index][head, pl.ds(own1 + block * n1, n1), :] = rows1
                low = HEADS * n1 + head * WHOLE
                whole[head] += got[low : low + WHOLE, cols(head)]
        for head in range(HEADS):
            if index == 2:
                nq[pl.ds(own3, WHOLE), cols(head)] = whole[head].astype(BF16)
            else:
                nkv[core, pl.ds(own2, WHOLE), cols(index * HEADS + head)] = whole[head].astype(BF16)

    def remote(src, dst, index, axis, peer):
        return pltpu.make_async_remote_copy(
            src_ref=src, dst_ref=dst, send_sem=send.at[index], recv_sem=recv.at[index],
            device_id={axis: peer}, device_id_type=mesh_id,
        )

    def slot(index):
        return pl.ds(pl.multiple_of(index * WHOLE, WHOLE), WHOLE)

    def key_copy(peer, index):
        return pltpu.make_async_remote_copy(
            src_ref=nkv.at[core, slot(inner)], dst_ref=nkv.at[core, slot(index)],
            send_sem=wk_send.at[peer], recv_sem=wk_recv.at[index],
            device_id={"inner": peer}, device_id_type=mesh_id,
        )

    def query_copy(peer, index):
        return pltpu.make_async_remote_copy(
            src_ref=nq.at[slot(chip)], dst_ref=nq.at[slot(index)],
            send_sem=wq_send.at[peer], recv_sem=wq_recv.at[index],
            device_id={"outer": peer * CORES + core}, device_id_type=mesh_id,
        )

    def result_copy(peer, index):
        return pltpu.make_async_remote_copy(
            src_ref=no_out.at[slot(peer)], dst_ref=no_in.at[slot(index)],
            send_sem=wo_send.at[peer], recv_sem=wo_recv.at[index],
            device_id={"outer": peer * CORES + core}, device_id_type=mesh_id,
        )

    core_copy = remote(nkv.at[core], nkv.at[core], 0, "outer", other_core)
    core_in = remote(nkv.at[1 - core], nkv.at[1 - core], 0, "outer", other_core)

    def each(first, last, act):
        def body(index, carry):
            act(index)
            return carry

        lax.fori_loop(first, last, body, 0)

    def each_key(act):
        each(1, GROUP, lambda step: act((inner + step) % GROUP))

    def each_earlier(act):
        each(0, chip, act)

    def each_later(act):
        each(chip + 1, CHIPS, act)

    flows = (
        (across, plane == 1, plane == 0),
        (diagonal, plane == 1, plane == 0),
        (reverse, y >= 2, y < 2),
    )
    pair_copies = []
    query_copies = []
    result_copies = []
    for head in range(HEADS):
        place = 1 + head * 8
        rows = pl.ds(own1, SEL)
        pair_copies.append(
            [
                remote(buffer.at[head, rows], buffer.at[head, rows], place + index, "inner", pair)
                for index, buffer in enumerate((gk, gv))
            ]
        )
        query_copies.append(
            [
                remote(gq.at[head], gqr.at[head, pl.ds(flow * SEL, SEL)], place + 2 + flow, "inner", peer)
                for flow, (peer, _, _) in enumerate(flows)
            ]
        )
        result_copies.append(
            [
                remote(gos.at[head, flow], gor.at[head, flow], place + 5 + flow, "inner", peer)
                for flow, (peer, _, _) in enumerate(flows)
            ]
        )

    def ask(head):
        @pl.when(plane == 1)
        def _():
            query_copies[head][1].start()
            query_copies[head][0].start()

        @pl.when(y >= 2)
        def _():
            query_copies[head][2].start()

    select(0)
    pl.semaphore_wait(barrier, GROUP - 1 + 1 + chip)
    pair_copies[0][0].start()
    select(1)
    pair_copies[0][1].start()
    each_key(lambda peer: key_copy(peer, inner).start())
    select(2)
    ask(0)
    each_earlier(lambda peer: query_copy(peer, chip).start())
    ask(1)
    pair_copies[1][0].start()
    pair_copies[1][1].start()

    for head in range(HEADS):
        vx[:, 2 * head * HD : (2 * head + 1) * HD] = v_ref[:, cols(head)]
        vx[:, (2 * head + 1) * HD : (2 * head + 2) * HD] = jnp.ones((ROWS, HD), BF16)

    def stored(block):
        rows = pl.ds(block * BQ, BQ)
        return pltpu.make_async_copy(att.at[rows], att_hbm.at[rows], store.at[block])

    def local(block):
        for head in range(HEADS):
            c = cols(head)
            out, lse = local_tile(q_ref, k_ref, vx, block, head)
            att[block * BQ : (block + 1) * BQ, c] = out.astype(BF16)
            out0[head, block * BQ : (block + 1) * BQ, :] = out
            lse0[head, block * BQ : (block + 1) * BQ, :] = lse
        stored(block).start()

    def group_foreign(head):
        for copy in pair_copies[head]:
            copy.wait_recv()

        def serve(first, count):
            for flow in range(first, first + count):
                query_copies[head][flow].wait_recv()
            out, lse = finish(dot_t(gqr[head, first * SEL : (first + count) * SEL, :], gk[head]), gv[head])
            for index in range(count):
                rows = slice(index * SEL, (index + 1) * SEL)
                gos[head, first + index, 0:SEL, :] = out[rows].astype(BF16)
                gos[head, first + index, SEL : SEL + 16, :] = pack_lse(lse[rows])
                result_copies[head][first + index].start()

        @pl.when(plane == 0)
        def _():
            serve(1, 1)
            serve(0, 1)

        @pl.when(y < 2)
        def _():
            serve(2, 1)

    def group_own(head):
        scores = dot_t(gq[head], gk[head])
        shape = (SEL, 2 * SEL)
        out, lse = finish(jnp.where(iota(shape, 1) <= iota(shape, 0) + own1, scores, NEG), gv[head])
        out1[head] = out
        lse1[head] = lse

    def group_merge(head):
        c = cols(head)
        for flow, (_, asks, _) in enumerate(flows):

            @pl.when(asks)
            def _():
                result_copies[head][flow].wait_recv()
                here = (out1[head], lse1[head])
                there = (gor[head, flow, 0:SEL, :].astype(F32), unpack_lse(gor[head, flow, SEL : SEL + 16, :]))
                out1[head], lse1[head] = merge([here, there])

    def whole_all():
        rows = CHIPS * WHOLE
        keys = CORES * GROUP * WHOLE
        shape = (rows, keys)
        row = iota(shape, 0)
        query_pos = (row // WHOLE * CORES + core) * GROUP * WHOLE + inner * WHOLE + row % WHOLE
        allowed = iota(shape, 1) + chip * keys <= query_pos
        place = iota((rows, HD), 1) // 16
        stats = jnp.zeros((rows, HD), F32)
        for head in range(HEADS):
            key_rows = nkv[:, :, cols(head)].reshape(keys, HD)
            value_rows = nkv[:, :, cols(HEADS + head)].reshape(keys, HD)
            out, lse = finish(jnp.where(allowed, dot_t(nq[:, cols(head)], key_rows), NEG), value_rows)
            no_out[:, cols(head)] = out.astype(BF16)
            stats = stats + three_terms(lse, place - 3 * head).astype(F32)
        no_out[:, cols(HEADS)] = stats.astype(BF16)
        no_in[slot(chip), :] = no_out[slot(chip), :]

    def whole_merge():
        each_earlier(lambda peer: result_copy(peer, peer).wait_recv())
        stats = no_in[:, cols(HEADS)].astype(F32)
        known = iota((CHIPS, WHOLE, HD), 0) <= chip
        merged = []
        for head in range(HEADS):
            parts = jnp.where(known, no_in[:, cols(head)].astype(F32).reshape(CHIPS, WHOLE, HD), 0.0)
            lane = 48 * head
            lse = stats[:, lane : lane + 1] + stats[:, lane + 16 : lane + 17] + stats[:, lane + 32 : lane + 33]
            lse = jnp.where(known, wide(lse, CHIPS * WHOLE).reshape(CHIPS, WHOLE, HD), NEG)
            top = jnp.max(lse, axis=0)
            weight = jnp.exp2(lse - top[None])
            total = jnp.sum(weight, axis=0)
            merged.append((jnp.sum(weight * parts, axis=0) / total, top + jnp.log2(total)))
        return merged

    def last_merge(head, whole):
        c = cols(head)
        group = (out1[head], lse1[head])
        rows = pl.ds(offs1[head], SEL, stride=GROUP)
        small[0:SEL, c] = merge([(out0[head, rows, :], lse0[head, rows, :]), group])[0]
        rows = pl.ds(offs2[head], WHOLE, stride=GROUP * GROUPS)
        rows1 = pl.ds(offs2[head] // GROUP, WHOLE, stride=GROUPS)
        same = jnp.full((WHOLE, HD), offs2[head] % GROUP) == offs1[head]
        lse = jnp.where(same, lse1[head, rows1, :], NEG)
        parts = [(out0[head, rows, :], lse0[head, rows, :]), (out1[head, rows1, :], lse), whole[head]]
        small[SEL : SEL + WHOLE, c] = merge(parts)[0]

    local(7)
    local(6)
    each_key(lambda peer: key_copy(peer, peer).wait_recv())
    core_copy.start()
    local(5)
    group_foreign(0)
    local(4)
    core_in.wait_recv()
    each_later(lambda peer: query_copy(peer, peer).wait_recv())
    whole_all()
    each_later(lambda peer: result_copy(peer, chip).start())
    group_foreign(1)
    group_own(0)
    group_own(1)
    local(3)
    local(2)
    local(1)
    local(0)
    whole = whole_merge()
    for head in range(HEADS):
        group_merge(head)
        last_merge(head, whole)
    last = pltpu.make_async_copy(small, small_hbm, store.at[BLOCKS])
    last.start()

    each_key(lambda peer: key_copy(peer, inner).wait_send())
    each_earlier(lambda peer: query_copy(peer, chip).wait_send())
    each_later(lambda peer: result_copy(peer, chip).wait_send())
    for block in range(BLOCKS):
        stored(block).wait()
    last.wait()
    core_copy.wait_send()
    for head in range(HEADS):
        for copy in pair_copies[head]:
            copy.wait_send()
        for flow, (_, asks, serves) in enumerate(flows):

            @pl.when(asks)
            def _():
                query_copies[head][flow].wait_send()

            @pl.when(serves)
            def _():
                result_copies[head][flow].wait_send()


SMALL = (SEL + WHOLE + 8, HEADS * HD)


def attention(queries, keys, values, offsets_group, offsets_global):
    hbm = pl.BlockSpec(memory_space=pltpu.HBM)
    dma = pltpu.SemaphoreType.DMA
    width = HEADS * HD
    return pl.pallas_call(
        attention_kernel,
        out_shape=[
            jax.ShapeDtypeStruct((ROWS, width), BF16),
            jax.ShapeDtypeStruct(SMALL, F32),
        ],
        in_specs=[hbm] * 5,
        out_specs=[hbm] * 2,
        scratch_shapes=[
            pltpu.SMEM((HEADS, GROUPS), jnp.int32),
            pltpu.SMEM((HEADS,), jnp.int32),
            pltpu.VMEM((ROWS, width), BF16),
            pltpu.VMEM((ROWS, width), BF16),
            pltpu.VMEM((ROWS, width), BF16),
            pltpu.VMEM((ROWS, 2 * width), BF16),
            pltpu.VMEM((ROWS, width), BF16),
            pltpu.VMEM(SMALL, F32),
            pltpu.VMEM((HEADS, ROWS, HD), F32),
            pltpu.VMEM((HEADS, ROWS, HD), F32),
            pltpu.VMEM((HEADS, SEL, HD), F32),
            pltpu.VMEM((HEADS, SEL, HD), F32),
            pltpu.VMEM((HEADS, 2 * SEL, HD), BF16),
            pltpu.VMEM((HEADS, 2 * SEL, HD), BF16),
            pltpu.VMEM((HEADS, SEL, HD), BF16),
            pltpu.VMEM((HEADS, 3 * SEL, HD), BF16),
            pltpu.VMEM((HEADS, 3, SEL + 16, HD), BF16),
            pltpu.VMEM((HEADS, 3, SEL + 16, HD), BF16),
            pltpu.VMEM((CORES, GROUP * WHOLE, 2 * width), BF16),
            pltpu.VMEM((CHIPS * WHOLE, width), BF16),
            pltpu.VMEM((CHIPS * WHOLE, width + HD), BF16),
            pltpu.VMEM((CHIPS * WHOLE, width + HD), BF16),
            dma((5,)),
            dma((BLOCKS + 1,)),
            dma((17,)),
            dma((17,)),
            dma((GROUP,)),
            dma((GROUP,)),
            dma((CHIPS,)),
            dma((CHIPS,)),
            dma((CHIPS,)),
            dma((CHIPS,)),
        ],
        compiler_params=pltpu.CompilerParams(
            collective_id=0, has_side_effects=True, vmem_limit_bytes=56 * 2**20
        ),
        cost_estimate=pl.CostEstimate(flops=5 * 10**9, bytes_accessed=4 * 2**20, transcendentals=6 * 10**6),
        name="attention",
    )(offsets_group.T, offsets_global, queries, keys, values)


SLOTS = 4


def project_kernel(att_hbm, small_hbm, w_hbm, o_ref, att, small, w_ref, buf, load, sem):
    def copy(block):
        return pltpu.make_async_copy(
            buf.at[block % SLOTS], o_ref.at[pl.ds(block * BQ, BQ)], sem.at[block % SLOTS]
        )

    def load_block(block):
        rows = pl.ds(block * BQ, BQ)
        return pltpu.make_async_copy(att_hbm.at[rows], att.at[rows], load.at[2 + block])

    w_copy = pltpu.make_async_copy(w_hbm, w_ref, load.at[1])
    small_copy = pltpu.make_async_copy(small_hbm, small, load.at[0])
    small_copy.start()
    load_block(0).start()
    w_copy.start()
    for block in range(1, BLOCKS):
        load_block(block).start()
    small_copy.wait()

    n1 = BQ // GROUP
    n2 = BQ // (GROUP * GROUPS)
    width = HEADS * HD
    spots = iota((BQ, width), 0)
    low = SEL + WHOLE
    left = iota((1, width), 1) < HD
    offset1 = jnp.where(left, small[low : low + 1, :], small[low + 1 : low + 2, :]).astype(jnp.int32)
    offset2 = jnp.where(left, small[low + 2 : low + 3, :], small[low + 3 : low + 4, :]).astype(jnp.int32)

    def spread(first, count):
        part = small[first : first + count, :]
        return jnp.broadcast_to(part[:, None, :], (count, BQ // count, width)).reshape(BQ, width)

    for block in range(BLOCKS):
        rows = slice(block * BQ, (block + 1) * BQ)
        load_block(block).wait()
        merged = jnp.where(spots % GROUP == offset1, spread(block * n1, n1), att[rows, :].astype(F32))
        merged = jnp.where(spots % (GROUP * GROUPS) == offset2, spread(SEL + block * n2, n2), merged).astype(BF16)
        if block == 0:
            w_copy.wait()
        if block >= SLOTS:
            copy(block - SLOTS).wait()
        buf[block % SLOTS] = dot(merged, w_ref[...]).astype(BF16)
        copy(block).start()
    for block in range(BLOCKS - SLOTS, BLOCKS):
        copy(block).wait()


def project(parts, weight):
    hbm = pl.BlockSpec(memory_space=pltpu.HBM)
    width = weight.shape[1]
    return pl.pallas_call(
        project_kernel,
        out_shape=jax.ShapeDtypeStruct((ROWS, width), BF16),
        in_specs=[hbm] * 3,
        out_specs=hbm,
        scratch_shapes=[
            pltpu.VMEM((ROWS, HEADS * HD), BF16),
            pltpu.VMEM(SMALL, F32),
            pltpu.VMEM((HEADS * HD, width), BF16),
            pltpu.VMEM((SLOTS, BQ, width), BF16),
            pltpu.SemaphoreType.DMA((2 + BLOCKS,)),
            pltpu.SemaphoreType.DMA((SLOTS,)),
        ],
        compiler_params=pltpu.CompilerParams(vmem_limit_bytes=56 * 2**20),
        cost_estimate=pl.CostEstimate(flops=43 * 10**8, bytes_accessed=19 * 2**20, transcendentals=0),
        name="project",
    )(*parts, weight)


def per_device(queries, keys, values, offsets_group, offsets_global, out_weight):
    return project(attention(queries, keys, values, offsets_group, offsets_global), out_weight)


def solution(mesh):
    rows = P(("outer", "inner"), None)
    return jax.shard_map(
        per_device, mesh=mesh, in_specs=(rows, rows, rows, P(), P(), P()), out_specs=rows, check_vma=False
    )
```

```python
import functools

import jax
import jax.numpy as jnp
from jax import lax
from jax.experimental import pallas as pl
from jax.experimental.pallas import tpu as pltpu
from jax.sharding import PartitionSpec as P

HD = 128
HEADS = 2
ROWS = 2048
RING = 4
PLANES = 2
GROUP = RING * PLANES
GROUPS = 16
CORES = 2
CHIPS = GROUPS // CORES
SEL = ROWS // GROUP
WHOLE = ROWS // (GROUP * GROUPS)
BQ = 256
BLOCKS = ROWS // BQ
SCALE = HD**-0.5 * 1.4426950408889634
NEG = -1e30
F32 = jnp.float32
BF16 = jnp.bfloat16


def iota(shape, dim):
    return lax.broadcasted_iota(jnp.int32, shape, dim)


def cols(head):
    return slice(head * HD, (head + 1) * HD)


def dot_t(a, b):
    return lax.dot_general(a, b, (((1,), (1,)), ((), ())), preferred_element_type=F32)


def dot(a, b):
    return jnp.dot(a, b, preferred_element_type=F32)


def wide(column, rows):
    return jnp.broadcast_to(column, (rows, HD))


def finish(scores, values):
    rows = scores.shape[0]
    top = jnp.max(scores, axis=1, keepdims=True)
    expo = jnp.exp2((scores - top) * SCALE)
    total = jnp.sum(expo, axis=1, keepdims=True)
    out = dot(expo.astype(BF16), values) / total
    return out, wide(top * SCALE + jnp.log2(total), rows)


def local_tile(q_ref, k_ref, vx_ref, block, head):
    low = block * BQ
    high = low + BQ
    scores = dot_t(q_ref[low:high, cols(head)], k_ref[0:high, cols(head)])
    diag = jnp.where(iota((BQ, BQ), 1) <= iota((BQ, BQ), 0), scores[:, low:], NEG)
    scores = diag if block == 0 else jnp.concatenate([scores[:, :low], diag], axis=1)
    top = jnp.max(scores, axis=1, keepdims=True)
    expo = jnp.exp2((scores - top) * SCALE)
    out = dot(expo.astype(BF16), vx_ref[0:high, head * 2 * HD : (head + 1) * 2 * HD])
    total = out[:, HD:]
    return out[:, :HD] / total, top * SCALE + jnp.log2(total)


def merge(parts):
    top = parts[0][1]
    for _, lse in parts[1:]:
        top = jnp.maximum(top, lse)
    weights = [jnp.exp2(lse - top) for _, lse in parts]
    out = sum(weight * part for weight, (part, _) in zip(weights, parts))
    total = sum(weights)
    return out / total, top + jnp.log2(total)


def three_terms(value, place):
    result = jnp.zeros(value.shape, F32)
    for term in range(3):
        head = value.astype(BF16).astype(F32)
        value = value - head
        result = jnp.where(place == term, head, result)
    return result.astype(BF16)


def pack_lse(lse):
    flat = lse.T[0:16, :]
    row = iota((16, HD), 0)
    return three_terms(jnp.where(row % 2 == 0, flat[:, :HD], flat[:, HD:]), row // 2)


def unpack_lse(packed):
    rows = packed.astype(F32)
    halves = [rows[h : h + 1] + rows[h + 2 : h + 3] + rows[h + 4 : h + 5] for h in range(2)]
    flat = jnp.concatenate(halves, axis=1)
    return jnp.broadcast_to(flat, (HD, SEL)).T


def attention_kernel(
    offg_hbm, offw_hbm, q_hbm, k_hbm, v_hbm,
    att_hbm, small_hbm,
    offg_ref, offw_ref, q_ref, k_ref, v_ref, vx, att, small, out0, lse0, out1, lse1,
    gk, gv, gq, gqr, gos, gor,
    nkv, nq, no_out, no_in,
    load, store, send, recv, wk_send, wk_recv, wq_send, wq_recv, wo_send, wo_recv,
):
    outer = lax.axis_index("outer")
    inner = lax.axis_index("inner")
    plane = inner // RING
    y = inner % RING
    chip = outer // CORES
    core = outer % CORES
    base = plane * RING
    pair = base + (y // 2) * 2 + 1 - y % 2
    across = (1 - plane) * RING + y
    reverse = base + RING - 1 - y
    diagonal = (1 - plane) * RING + RING - 1 - y
    other_core = chip * CORES + 1 - core
    mesh_id = pl.DeviceIdType.MESH

    barrier = pltpu.get_barrier_semaphore()

    def greet_inner(step, carry):
        pl.semaphore_signal(barrier, inc=1, device_id={"inner": (inner + step) % GROUP}, device_id_type=mesh_id)
        return carry

    def greet_outer(peer, carry):
        pl.semaphore_signal(barrier, inc=1, device_id={"outer": peer * CORES + core}, device_id_type=mesh_id)
        return carry

    lax.fori_loop(1, GROUP, greet_inner, 0)
    lax.fori_loop(chip + 1, CHIPS, greet_outer, 0)
    pl.semaphore_signal(barrier, inc=1, device_id={"outer": other_core}, device_id_type=mesh_id)

    loads = [
        pltpu.make_async_copy(src, dst, load.at[index])
        for index, (src, dst) in enumerate(
            ((offg_hbm, offg_ref), (offw_hbm, offw_ref), (k_hbm, k_ref), (v_hbm, v_ref), (q_hbm, q_ref))
        )
    ]
    for copy in loads:
        copy.start()
    loads[0].wait()
    loads[1].wait()

    offs1 = [offg_ref[head, outer] for head in range(HEADS)]
    offs2 = [offw_ref[head] for head in range(HEADS)]
    row8 = iota((8, HD), 0)
    offsets = jnp.where(
        row8 == 0, offs1[0], jnp.where(row8 == 1, offs1[1], jnp.where(row8 == 2, offs2[0], offs2[1]))
    )
    for head in range(HEADS):
        small[SEL + WHOLE : SEL + WHOLE + 8, cols(head)] = offsets.astype(F32)
    n1 = BQ // GROUP
    pick1 = [
        (iota((n1, BQ), 1) == iota((n1, BQ), 0) * GROUP + offs1[head]).astype(F32).astype(BF16)
        for head in range(HEADS)
    ]
    picks = []
    for block in range(BLOCKS):
        pick2 = [
            (iota((WHOLE, BQ), 1) + block * BQ == iota((WHOLE, BQ), 0) * (GROUP * GROUPS) + offs2[head])
            .astype(F32).astype(BF16)
            for head in range(HEADS)
        ]
        picks.append(jnp.concatenate(pick1 + pick2, axis=0))
    own1 = pl.multiple_of((y % 2) * SEL, SEL)
    own2 = pl.multiple_of(inner * WHOLE, WHOLE)
    own3 = pl.multiple_of(chip * WHOLE, WHOLE)
    def select(index):
        ref = (k_ref, v_ref, q_ref)[index]
        loads[2 + index].wait()
        whole = [jnp.zeros((WHOLE, HD), F32) for _ in range(HEADS)]
        for block in range(BLOCKS):
            got = dot(picks[block], ref[block * BQ : (block + 1) * BQ, :])
            for head in range(HEADS):
                rows1 = got[head * n1 : (head + 1) * n1, cols(head)].astype(BF16)
                if index == 2:
                    gq[head, block * n1 : (block + 1) * n1, :] = rows1
                else:
                    (gk, gv)[index][head, pl.ds(own1 + block * n1, n1), :] = rows1
                low = HEADS * n1 + head * WHOLE
                whole[head] += got[low : low + WHOLE, cols(head)]
        for head in range(HEADS):
            if index == 2:
                nq[pl.ds(own3, WHOLE), cols(head)] = whole[head].astype(BF16)
            else:
                nkv[core, pl.ds(own2, WHOLE), cols(index * HEADS + head)] = whole[head].astype(BF16)

    def remote(src, dst, index, axis, peer):
        return pltpu.make_async_remote_copy(
            src_ref=src, dst_ref=dst, send_sem=send.at[index], recv_sem=recv.at[index],
            device_id={axis: peer}, device_id_type=mesh_id,
        )

    def slot(index):
        return pl.ds(pl.multiple_of(index * WHOLE, WHOLE), WHOLE)

    def key_copy(peer, index):
        return pltpu.make_async_remote_copy(
            src_ref=nkv.at[core, slot(inner)], dst_ref=nkv.at[core, slot(index)],
            send_sem=wk_send.at[peer], recv_sem=wk_recv.at[index],
            device_id={"inner": peer}, device_id_type=mesh_id,
        )

    def query_copy(peer, index):
        return pltpu.make_async_remote_copy(
            src_ref=nq.at[slot(chip)], dst_ref=nq.at[slot(index)],
            send_sem=wq_send.at[peer], recv_sem=wq_recv.at[index],
            device_id={"outer": peer * CORES + core}, device_id_type=mesh_id,
        )

    def result_copy(peer, index):
        return pltpu.make_async_remote_copy(
            src_ref=no_out.at[slot(peer)], dst_ref=no_in.at[slot(index)],
            send_sem=wo_send.at[peer], recv_sem=wo_recv.at[index],
            device_id={"outer": peer * CORES + core}, device_id_type=mesh_id,
        )

    core_copy = remote(nkv.at[core], nkv.at[core], 0, "outer", other_core)
    core_in = remote(nkv.at[1 - core], nkv.at[1 - core], 0, "outer", other_core)

    def each(first, last, act):
        def body(index, carry):
            act(index)
            return carry

        lax.fori_loop(first, last, body, 0)

    def each_key(act):
        each(1, GROUP, lambda step: act((inner + step) % GROUP))

    def each_earlier(act):
        each(0, chip, act)

    def each_later(act):
        each(chip + 1, CHIPS, act)

    flows = (
        (across, plane == 1, plane == 0),
        (diagonal, plane == 1, plane == 0),
        (reverse, y >= 2, y < 2),
    )
    pair_copies = []
    query_copies = []
    result_copies = []
    for head in range(HEADS):
        place = 1 + head * 8
        rows = pl.ds(own1, SEL)
        pair_copies.append(
            [
                remote(buffer.at[head, rows], buffer.at[head, rows], place + index, "inner", pair)
                for index, buffer in enumerate((gk, gv))
            ]
        )
        query_copies.append(
            [
                remote(gq.at[head], gqr.at[head, pl.ds(flow * SEL, SEL)], place + 2 + flow, "inner", peer)
                for flow, (peer, _, _) in enumerate(flows)
            ]
        )
        result_copies.append(
            [
                remote(gos.at[head, flow], gor.at[head, flow], place + 5 + flow, "inner", peer)
                for flow, (peer, _, _) in enumerate(flows)
            ]
        )

    def ask(head):
        @pl.when(plane == 1)
        def _():
            query_copies[head][1].start()
            query_copies[head][0].start()

        @pl.when(y >= 2)
        def _():
            query_copies[head][2].start()

    select(0)
    select(1)
    pl.semaphore_wait(barrier, GROUP - 1 + 1 + chip)
    each_key(lambda peer: key_copy(peer, inner).start())
    pair_copies[0][0].start()
    pair_copies[0][1].start()
    select(2)
    ask(0)
    each_earlier(lambda peer: query_copy(peer, chip).start())

    for head in range(HEADS):
        vx[:, 2 * head * HD : (2 * head + 1) * HD] = v_ref[:, cols(head)]
        vx[:, (2 * head + 1) * HD : (2 * head + 2) * HD] = jnp.ones((ROWS, HD), BF16)

    def stored(block):
        rows = pl.ds(block * BQ, BQ)
        return pltpu.make_async_copy(att.at[rows], att_hbm.at[rows], store.at[block])

    def local(block):
        for head in range(HEADS):
            c = cols(head)
            out, lse = local_tile(q_ref, k_ref, vx, block, head)
            att[block * BQ : (block + 1) * BQ, c] = out.astype(BF16)
            out0[head, block * BQ : (block + 1) * BQ, :] = out
            lse0[head, block * BQ : (block + 1) * BQ, :] = lse
        stored(block).start()

    def group_foreign(head):
        def serve(first, count):
            for flow in range(first, first + count):
                query_copies[head][flow].wait_recv()
            out, lse = finish(dot_t(gqr[head, first * SEL : (first + count) * SEL, :], gk[head]), gv[head])
            for index in range(count):
                rows = slice(index * SEL, (index + 1) * SEL)
                gos[head, first + index, 0:SEL, :] = out[rows].astype(BF16)
                gos[head, first + index, SEL : SEL + 16, :] = pack_lse(lse[rows])
                result_copies[head][first + index].start()

        @pl.when(plane == 0)
        def _():
            serve(1, 1)
            serve(0, 1)

        @pl.when(y < 2)
        def _():
            serve(2, 1)

    def pair_wait(head):
        for copy in pair_copies[head]:
            copy.wait_recv()

    def group_own(head):
        scores = dot_t(gq[head], gk[head])
        shape = (SEL, 2 * SEL)
        out, lse = finish(jnp.where(iota(shape, 1) <= iota(shape, 0) + own1, scores, NEG), gv[head])
        out1[head] = out
        lse1[head] = lse

    def group_merge(head):
        c = cols(head)
        for flow, (_, asks, _) in enumerate(flows):

            @pl.when(asks)
            def _():
                result_copies[head][flow].wait_recv()
                here = (out1[head], lse1[head])
                there = (gor[head, flow, 0:SEL, :].astype(F32), unpack_lse(gor[head, flow, SEL : SEL + 16, :]))
                out1[head], lse1[head] = merge([here, there])

    def whole_all():
        rows = CHIPS * WHOLE
        keys = CORES * GROUP * WHOLE
        shape = (rows, keys)
        row = iota(shape, 0)
        query_pos = (row // WHOLE * CORES + core) * GROUP * WHOLE + inner * WHOLE + row % WHOLE
        allowed = iota(shape, 1) + chip * keys <= query_pos
        place = iota((rows, HD), 1) // 16
        stats = jnp.zeros((rows, HD), F32)
        for head in range(HEADS):
            key_rows = nkv[:, :, cols(head)].reshape(keys, HD)
            value_rows = nkv[:, :, cols(HEADS + head)].reshape(keys, HD)
            out, lse = finish(jnp.where(allowed, dot_t(nq[:, cols(head)], key_rows), NEG), value_rows)
            no_out[:, cols(head)] = out.astype(BF16)
            stats = stats + three_terms(lse, place - 3 * head).astype(F32)
        no_out[:, cols(HEADS)] = stats.astype(BF16)
        no_in[slot(chip), :] = no_out[slot(chip), :]

    def whole_merge():
        each_earlier(lambda peer: result_copy(peer, peer).wait_recv())
        stats = no_in[:, cols(HEADS)].astype(F32)
        known = iota((CHIPS, WHOLE, HD), 0) <= chip
        merged = []
        for head in range(HEADS):
            parts = jnp.where(known, no_in[:, cols(head)].astype(F32).reshape(CHIPS, WHOLE, HD), 0.0)
            lane = 48 * head
            lse = stats[:, lane : lane + 1] + stats[:, lane + 16 : lane + 17] + stats[:, lane + 32 : lane + 33]
            lse = jnp.where(known, wide(lse, CHIPS * WHOLE).reshape(CHIPS, WHOLE, HD), NEG)
            top = jnp.max(lse, axis=0)
            weight = jnp.exp2(lse - top[None])
            total = jnp.sum(weight, axis=0)
            merged.append((jnp.sum(weight * parts, axis=0) / total, top + jnp.log2(total)))
        return merged

    def last_merge(head, whole):
        c = cols(head)
        group = (out1[head], lse1[head])
        rows = pl.ds(offs1[head], SEL, stride=GROUP)
        small[0:SEL, c] = merge([(out0[head, rows, :], lse0[head, rows, :]), group])[0]
        rows = pl.ds(offs2[head], WHOLE, stride=GROUP * GROUPS)
        rows1 = pl.ds(offs2[head] // GROUP, WHOLE, stride=GROUPS)
        same = jnp.full((WHOLE, HD), offs2[head] % GROUP) == offs1[head]
        lse = jnp.where(same, lse1[head, rows1, :], NEG)
        parts = [(out0[head, rows, :], lse0[head, rows, :]), (out1[head, rows1, :], lse), whole[head]]
        small[SEL : SEL + WHOLE, c] = merge(parts)[0]

    local(7)
    local(6)
    ask(1)
    pair_copies[1][0].start()
    pair_copies[1][1].start()
    local(5)
    local(4)
    each_key(lambda peer: key_copy(peer, peer).wait_recv())
    core_copy.start()
    pair_wait(0)
    group_own(0)
    group_foreign(0)
    local(3)
    core_in.wait_recv()
    each_later(lambda peer: query_copy(peer, peer).wait_recv())
    whole_all()
    each_later(lambda peer: result_copy(peer, chip).start())
    pair_wait(1)
    group_foreign(1)
    group_own(1)
    local(2)
    local(1)
    local(0)
    whole = whole_merge()
    for head in range(HEADS):
        group_merge(head)
        last_merge(head, whole)
    last = pltpu.make_async_copy(small, small_hbm, store.at[BLOCKS])
    last.start()

    each_key(lambda peer: key_copy(peer, inner).wait_send())
    each_earlier(lambda peer: query_copy(peer, chip).wait_send())
    each_later(lambda peer: result_copy(peer, chip).wait_send())
    for block in range(BLOCKS):
        stored(block).wait()
    last.wait()
    core_copy.wait_send()
    for head in range(HEADS):
        for copy in pair_copies[head]:
            copy.wait_send()
        for flow, (_, asks, serves) in enumerate(flows):

            @pl.when(asks)
            def _():
                query_copies[head][flow].wait_send()

            @pl.when(serves)
            def _():
                result_copies[head][flow].wait_send()


SMALL = (SEL + WHOLE + 8, HEADS * HD)


def attention(queries, keys, values, offsets_group, offsets_global):
    hbm = pl.BlockSpec(memory_space=pltpu.HBM)
    dma = pltpu.SemaphoreType.DMA
    width = HEADS * HD
    return pl.pallas_call(
        attention_kernel,
        out_shape=[
            jax.ShapeDtypeStruct((ROWS, width), BF16),
            jax.ShapeDtypeStruct(SMALL, F32),
        ],
        in_specs=[hbm] * 5,
        out_specs=[hbm] * 2,
        scratch_shapes=[
            pltpu.SMEM((HEADS, GROUPS), jnp.int32),
            pltpu.SMEM((HEADS,), jnp.int32),
            pltpu.VMEM((ROWS, width), BF16),
            pltpu.VMEM((ROWS, width), BF16),
            pltpu.VMEM((ROWS, width), BF16),
            pltpu.VMEM((ROWS, 2 * width), BF16),
            pltpu.VMEM((ROWS, width), BF16),
            pltpu.VMEM(SMALL, F32),
            pltpu.VMEM((HEADS, ROWS, HD), F32),
            pltpu.VMEM((HEADS, ROWS, HD), F32),
            pltpu.VMEM((HEADS, SEL, HD), F32),
            pltpu.VMEM((HEADS, SEL, HD), F32),
            pltpu.VMEM((HEADS, 2 * SEL, HD), BF16),
            pltpu.VMEM((HEADS, 2 * SEL, HD), BF16),
            pltpu.VMEM((HEADS, SEL, HD), BF16),
            pltpu.VMEM((HEADS, 3 * SEL, HD), BF16),
            pltpu.VMEM((HEADS, 3, SEL + 16, HD), BF16),
            pltpu.VMEM((HEADS, 3, SEL + 16, HD), BF16),
            pltpu.VMEM((CORES, GROUP * WHOLE, 2 * width), BF16),
            pltpu.VMEM((CHIPS * WHOLE, width), BF16),
            pltpu.VMEM((CHIPS * WHOLE, width + HD), BF16),
            pltpu.VMEM((CHIPS * WHOLE, width + HD), BF16),
            dma((5,)),
            dma((BLOCKS + 1,)),
            dma((17,)),
            dma((17,)),
            dma((GROUP,)),
            dma((GROUP,)),
            dma((CHIPS,)),
            dma((CHIPS,)),
            dma((CHIPS,)),
            dma((CHIPS,)),
        ],
        compiler_params=pltpu.CompilerParams(
            collective_id=0, has_side_effects=True, vmem_limit_bytes=56 * 2**20
        ),
        cost_estimate=pl.CostEstimate(flops=5 * 10**9, bytes_accessed=4 * 2**20, transcendentals=6 * 10**6),
        name="attention",
    )(offsets_group.T, offsets_global, queries, keys, values)


SLOTS = 4


def project_kernel(att_hbm, small_hbm, w_hbm, o_ref, att, small, w_ref, buf, load, sem):
    def copy(block):
        return pltpu.make_async_copy(
            buf.at[block % SLOTS], o_ref.at[pl.ds(block * BQ, BQ)], sem.at[block % SLOTS]
        )

    def load_block(block):
        rows = pl.ds(block * BQ, BQ)
        return pltpu.make_async_copy(att_hbm.at[rows], att.at[rows], load.at[2 + block])

    w_copy = pltpu.make_async_copy(w_hbm, w_ref, load.at[1])
    small_copy = pltpu.make_async_copy(small_hbm, small, load.at[0])
    small_copy.start()
    load_block(0).start()
    w_copy.start()
    for block in range(1, BLOCKS):
        load_block(block).start()
    small_copy.wait()

    n1 = BQ // GROUP
    n2 = BQ // (GROUP * GROUPS)
    width = HEADS * HD
    spots = iota((BQ, width), 0)
    low = SEL + WHOLE
    left = iota((1, width), 1) < HD
    offset1 = jnp.where(left, small[low : low + 1, :], small[low + 1 : low + 2, :]).astype(jnp.int32)
    offset2 = jnp.where(left, small[low + 2 : low + 3, :], small[low + 3 : low + 4, :]).astype(jnp.int32)

    def spread(first, count):
        part = small[first : first + count, :]
        return jnp.broadcast_to(part[:, None, :], (count, BQ // count, width)).reshape(BQ, width)

    for block in range(BLOCKS):
        rows = slice(block * BQ, (block + 1) * BQ)
        load_block(block).wait()
        merged = jnp.where(spots % GROUP == offset1, spread(block * n1, n1), att[rows, :].astype(F32))
        merged = jnp.where(spots % (GROUP * GROUPS) == offset2, spread(SEL + block * n2, n2), merged).astype(BF16)
        if block == 0:
            w_copy.wait()
        if block >= SLOTS:
            copy(block - SLOTS).wait()
        buf[block % SLOTS] = dot(merged, w_ref[...]).astype(BF16)
        copy(block).start()
    for block in range(BLOCKS - SLOTS, BLOCKS):
        copy(block).wait()


def project(parts, weight):
    hbm = pl.BlockSpec(memory_space=pltpu.HBM)
    width = weight.shape[1]
    return pl.pallas_call(
        project_kernel,
        out_shape=jax.ShapeDtypeStruct((ROWS, width), BF16),
        in_specs=[hbm] * 3,
        out_specs=hbm,
        scratch_shapes=[
            pltpu.VMEM((ROWS, HEADS * HD), BF16),
            pltpu.VMEM(SMALL, F32),
            pltpu.VMEM((HEADS * HD, width), BF16),
            pltpu.VMEM((SLOTS, BQ, width), BF16),
            pltpu.SemaphoreType.DMA((2 + BLOCKS,)),
            pltpu.SemaphoreType.DMA((SLOTS,)),
        ],
        compiler_params=pltpu.CompilerParams(vmem_limit_bytes=56 * 2**20),
        cost_estimate=pl.CostEstimate(flops=43 * 10**8, bytes_accessed=19 * 2**20, transcendentals=0),
        name="project",
    )(*parts, weight)


def per_device(queries, keys, values, offsets_group, offsets_global, out_weight):
    return project(attention(queries, keys, values, offsets_group, offsets_global), out_weight)


def solution(mesh):
    rows = P(("outer", "inner"), None)
    return jax.shard_map(
        per_device, mesh=mesh, in_specs=(rows, rows, rows, P(), P(), P()), out_specs=rows, check_vma=False
    )
```

```python
import functools

import jax
import jax.numpy as jnp
from jax import lax
from jax.experimental import pallas as pl
from jax.experimental.pallas import tpu as pltpu
from jax.sharding import PartitionSpec as P

HD = 128
HEADS = 2
ROWS = 2048
RING = 4
PLANES = 2
GROUP = RING * PLANES
GROUPS = 16
CORES = 2
CHIPS = GROUPS // CORES
SEL = ROWS // GROUP
WHOLE = ROWS // (GROUP * GROUPS)
BQ = 256
BLOCKS = ROWS // BQ
SCALE = HD**-0.5 * 1.4426950408889634
NEG = -1e30
F32 = jnp.float32
BF16 = jnp.bfloat16


def iota(shape, dim):
    return lax.broadcasted_iota(jnp.int32, shape, dim)


def cols(head):
    return slice(head * HD, (head + 1) * HD)


def dot_t(a, b):
    return lax.dot_general(a, b, (((1,), (1,)), ((), ())), preferred_element_type=F32)


def dot(a, b):
    return jnp.dot(a, b, preferred_element_type=F32)


def wide(column, rows):
    return jnp.broadcast_to(column, (rows, HD))


def finish(scores, values):
    rows = scores.shape[0]
    top = jnp.max(scores, axis=1, keepdims=True)
    expo = jnp.exp2((scores - top) * SCALE)
    total = jnp.sum(expo, axis=1, keepdims=True)
    out = dot(expo.astype(BF16), values) / total
    return out, wide(top * SCALE + jnp.log2(total), rows)


def local_tile(q_ref, k_ref, vx_ref, block, head):
    low = block * BQ
    high = low + BQ
    scores = dot_t(q_ref[low:high, cols(head)], k_ref[0:high, cols(head)])
    diag = jnp.where(iota((BQ, BQ), 1) <= iota((BQ, BQ), 0), scores[:, low:], NEG)
    scores = diag if block == 0 else jnp.concatenate([scores[:, :low], diag], axis=1)
    top = jnp.max(scores, axis=1, keepdims=True)
    expo = jnp.exp2((scores - top) * SCALE)
    out = dot(expo.astype(BF16), vx_ref[0:high, head * 2 * HD : (head + 1) * 2 * HD])
    total = out[:, HD:]
    return out[:, :HD] / total, top * SCALE + jnp.log2(total)


def merge(parts):
    top = parts[0][1]
    for _, lse in parts[1:]:
        top = jnp.maximum(top, lse)
    weights = [jnp.exp2(lse - top) for _, lse in parts]
    out = sum(weight * part for weight, (part, _) in zip(weights, parts))
    total = sum(weights)
    return out / total, top + jnp.log2(total)


def three_terms(value, place):
    result = jnp.zeros(value.shape, F32)
    for term in range(3):
        head = value.astype(BF16).astype(F32)
        value = value - head
        result = jnp.where(place == term, head, result)
    return result.astype(BF16)


def pack_lse(lse):
    flat = lse.T[0:16, :]
    row = iota((16, HD), 0)
    return three_terms(jnp.where(row % 2 == 0, flat[:, :HD], flat[:, HD:]), row // 2)


def unpack_lse(packed):
    rows = packed.astype(F32)
    halves = [rows[h : h + 1] + rows[h + 2 : h + 3] + rows[h + 4 : h + 5] for h in range(2)]
    flat = jnp.concatenate(halves, axis=1)
    return jnp.broadcast_to(flat, (HD, SEL)).T


def attention_kernel(
    offg_hbm, offw_hbm, q_hbm, k_hbm, v_hbm,
    att_hbm, small_hbm,
    offg_ref, offw_ref, q_ref, k_ref, v_ref, vx, att, small, out0, lse0, out1, lse1,
    gk, gv, gq, gqr, gos, gor,
    nkv, nq, no_out, no_in,
    load, store, send, recv, wk_send, wk_recv, wq_send, wq_recv, wo_send, wo_recv,
):
    outer = lax.axis_index("outer")
    inner = lax.axis_index("inner")
    plane = inner // RING
    y = inner % RING
    chip = outer // CORES
    core = outer % CORES
    base = plane * RING
    pair = base + (y // 2) * 2 + 1 - y % 2
    across = (1 - plane) * RING + y
    reverse = base + RING - 1 - y
    diagonal = (1 - plane) * RING + RING - 1 - y
    other_core = chip * CORES + 1 - core
    mesh_id = pl.DeviceIdType.MESH

    barrier = pltpu.get_barrier_semaphore()

    def greet_inner(step, carry):
        pl.semaphore_signal(barrier, inc=1, device_id={"inner": (inner + step) % GROUP}, device_id_type=mesh_id)
        return carry

    def greet_outer(peer, carry):
        pl.semaphore_signal(barrier, inc=1, device_id={"outer": peer * CORES + core}, device_id_type=mesh_id)
        return carry

    lax.fori_loop(1, GROUP, greet_inner, 0)
    lax.fori_loop(chip + 1, CHIPS, greet_outer, 0)
    pl.semaphore_signal(barrier, inc=1, device_id={"outer": other_core}, device_id_type=mesh_id)

    loads = [
        pltpu.make_async_copy(src, dst, load.at[index])
        for index, (src, dst) in enumerate(
            ((offg_hbm, offg_ref), (offw_hbm, offw_ref), (k_hbm, k_ref), (v_hbm, v_ref), (q_hbm, q_ref))
        )
    ]
    for copy in loads:
        copy.start()
    loads[0].wait()
    loads[1].wait()

    offs1 = [offg_ref[head, outer] for head in range(HEADS)]
    offs2 = [offw_ref[head] for head in range(HEADS)]
    row8 = iota((8, HD), 0)
    offsets = jnp.where(
        row8 == 0, offs1[0], jnp.where(row8 == 1, offs1[1], jnp.where(row8 == 2, offs2[0], offs2[1]))
    )
    for head in range(HEADS):
        small[SEL + WHOLE : SEL + WHOLE + 8, cols(head)] = offsets.astype(F32)
    n1 = BQ // GROUP
    pick1 = [
        (iota((n1, BQ), 1) == iota((n1, BQ), 0) * GROUP + offs1[head]).astype(F32).astype(BF16)
        for head in range(HEADS)
    ]
    picks = []
    for block in range(BLOCKS):
        pick2 = [
            (iota((WHOLE, BQ), 1) + block * BQ == iota((WHOLE, BQ), 0) * (GROUP * GROUPS) + offs2[head])
            .astype(F32).astype(BF16)
            for head in range(HEADS)
        ]
        picks.append(jnp.concatenate(pick1 + pick2, axis=0))
    own1 = pl.multiple_of((y % 2) * SEL, SEL)
    own2 = pl.multiple_of(inner * WHOLE, WHOLE)
    own3 = pl.multiple_of(chip * WHOLE, WHOLE)
    def select(index):
        ref = (k_ref, v_ref, q_ref)[index]
        loads[2 + index].wait()
        whole = [jnp.zeros((WHOLE, HD), F32) for _ in range(HEADS)]
        for block in range(BLOCKS):
            got = dot(picks[block], ref[block * BQ : (block + 1) * BQ, :])
            for head in range(HEADS):
                rows1 = got[head * n1 : (head + 1) * n1, cols(head)].astype(BF16)
                if index == 2:
                    gq[head, block * n1 : (block + 1) * n1, :] = rows1
                else:
                    (gk, gv)[index][head, pl.ds(own1 + block * n1, n1), :] = rows1
                low = HEADS * n1 + head * WHOLE
                whole[head] += got[low : low + WHOLE, cols(head)]
        for head in range(HEADS):
            if index == 2:
                nq[pl.ds(own3, WHOLE), cols(head)] = whole[head].astype(BF16)
            else:
                nkv[core, pl.ds(own2, WHOLE), cols(index * HEADS + head)] = whole[head].astype(BF16)

    def remote(src, dst, index, axis, peer):
        return pltpu.make_async_remote_copy(
            src_ref=src, dst_ref=dst, send_sem=send.at[index], recv_sem=recv.at[index],
            device_id={axis: peer}, device_id_type=mesh_id,
        )

    def slot(index):
        return pl.ds(pl.multiple_of(index * WHOLE, WHOLE), WHOLE)

    def key_copy(peer, index):
        return pltpu.make_async_remote_copy(
            src_ref=nkv.at[core, slot(inner)], dst_ref=nkv.at[core, slot(index)],
            send_sem=wk_send.at[peer], recv_sem=wk_recv.at[index],
            device_id={"inner": peer}, device_id_type=mesh_id,
        )

    def query_copy(peer, index):
        return pltpu.make_async_remote_copy(
            src_ref=nq.at[slot(chip)], dst_ref=nq.at[slot(index)],
            send_sem=wq_send.at[peer], recv_sem=wq_recv.at[index],
            device_id={"outer": peer * CORES + core}, device_id_type=mesh_id,
        )

    def result_copy(peer, index):
        return pltpu.make_async_remote_copy(
            src_ref=no_out.at[slot(peer)], dst_ref=no_in.at[slot(index)],
            send_sem=wo_send.at[peer], recv_sem=wo_recv.at[index],
            device_id={"outer": peer * CORES + core}, device_id_type=mesh_id,
        )

    core_copy = remote(nkv.at[core], nkv.at[core], 0, "outer", other_core)
    core_in = remote(nkv.at[1 - core], nkv.at[1 - core], 0, "outer", other_core)

    def each(first, last, act):
        def body(index, carry):
            act(index)
            return carry

        lax.fori_loop(first, last, body, 0)

    def each_key(act):
        each(1, GROUP, lambda step: act((inner + step) % GROUP))

    def each_earlier(act):
        each(0, chip, act)

    def each_later(act):
        each(chip + 1, CHIPS, act)

    flows = (
        (across, plane == 1, plane == 0),
        (diagonal, plane == 1, plane == 0),
        (reverse, y >= 2, y < 2),
    )
    pair_copies = []
    query_copies = []
    result_copies = []
    for head in range(HEADS):
        place = 1 + head * 8
        rows = pl.ds(own1, SEL)
        pair_copies.append(
            [
                remote(buffer.at[head, rows], buffer.at[head, rows], place + index, "inner", pair)
                for index, buffer in enumerate((gk, gv))
            ]
        )
        query_copies.append(
            [
                remote(gq.at[head], gqr.at[head, pl.ds(flow * SEL, SEL)], place + 2 + flow, "inner", peer)
                for flow, (peer, _, _) in enumerate(flows)
            ]
        )
        result_copies.append(
            [
                remote(gos.at[head, flow], gor.at[head, flow], place + 5 + flow, "inner", peer)
                for flow, (peer, _, _) in enumerate(flows)
            ]
        )

    def ask(head):
        @pl.when(plane == 1)
        def _():
            query_copies[head][1].start()
            query_copies[head][0].start()

        @pl.when(y >= 2)
        def _():
            query_copies[head][2].start()

    select(0)
    select(1)
    pl.semaphore_wait(barrier, GROUP - 1 + 1 + chip)
    each_key(lambda peer: key_copy(peer, inner).start())
    pair_copies[0][0].start()
    pair_copies[0][1].start()
    select(2)
    ask(0)
    each_earlier(lambda peer: query_copy(peer, chip).start())

    for head in range(HEADS):
        vx[:, 2 * head * HD : (2 * head + 1) * HD] = v_ref[:, cols(head)]
        vx[:, (2 * head + 1) * HD : (2 * head + 2) * HD] = jnp.ones((ROWS, HD), BF16)

    def stored(block):
        rows = pl.ds(block * BQ, BQ)
        return pltpu.make_async_copy(att.at[rows], att_hbm.at[rows], store.at[block])

    def local(block):
        for head in range(HEADS):
            c = cols(head)
            out, lse = local_tile(q_ref, k_ref, vx, block, head)
            att[block * BQ : (block + 1) * BQ, c] = out.astype(BF16)
            out0[head, block * BQ : (block + 1) * BQ, :] = out
            lse0[head, block * BQ : (block + 1) * BQ, :] = lse
        stored(block).start()

    def group_foreign(head):
        def serve(first, count):
            for flow in range(first, first + count):
                query_copies[head][flow].wait_recv()
            out, lse = finish(dot_t(gqr[head, first * SEL : (first + count) * SEL, :], gk[head]), gv[head])
            for index in range(count):
                rows = slice(index * SEL, (index + 1) * SEL)
                gos[head, first + index, 0:SEL, :] = out[rows].astype(BF16)
                gos[head, first + index, SEL : SEL + 16, :] = pack_lse(lse[rows])
                result_copies[head][first + index].start()

        @pl.when(plane == 0)
        def _():
            serve(1, 1)
            serve(0, 1)

        @pl.when(y < 2)
        def _():
            serve(2, 1)

    def pair_wait(head):
        for copy in pair_copies[head]:
            copy.wait_recv()

    def group_own(head):
        scores = dot_t(gq[head], gk[head])
        shape = (SEL, 2 * SEL)
        out, lse = finish(jnp.where(iota(shape, 1) <= iota(shape, 0) + own1, scores, NEG), gv[head])
        out1[head] = out
        lse1[head] = lse

    def group_merge(head):
        c = cols(head)
        for flow, (_, asks, _) in enumerate(flows):

            @pl.when(asks)
            def _():
                result_copies[head][flow].wait_recv()
                here = (out1[head], lse1[head])
                there = (gor[head, flow, 0:SEL, :].astype(F32), unpack_lse(gor[head, flow, SEL : SEL + 16, :]))
                out1[head], lse1[head] = merge([here, there])

    def whole_all():
        rows = CHIPS * WHOLE
        keys = CORES * GROUP * WHOLE
        shape = (rows, keys)
        row = iota(shape, 0)
        query_pos = (row // WHOLE * CORES + core) * GROUP * WHOLE + inner * WHOLE + row % WHOLE
        allowed = iota(shape, 1) + chip * keys <= query_pos
        place = iota((rows, HD), 1) // 16
        stats = jnp.zeros((rows, HD), F32)
        for head in range(HEADS):
            key_rows = nkv[:, :, cols(head)].reshape(keys, HD)
            value_rows = nkv[:, :, cols(HEADS + head)].reshape(keys, HD)
            out, lse = finish(jnp.where(allowed, dot_t(nq[:, cols(head)], key_rows), NEG), value_rows)
            no_out[:, cols(head)] = out.astype(BF16)
            stats = stats + three_terms(lse, place - 3 * head).astype(F32)
        no_out[:, cols(HEADS)] = stats.astype(BF16)
        no_in[slot(chip), :] = no_out[slot(chip), :]

    def whole_merge():
        each_earlier(lambda peer: result_copy(peer, peer).wait_recv())
        stats = no_in[:, cols(HEADS)].astype(F32)
        known = iota((CHIPS, WHOLE, HD), 0) <= chip
        merged = []
        for head in range(HEADS):
            parts = jnp.where(known, no_in[:, cols(head)].astype(F32).reshape(CHIPS, WHOLE, HD), 0.0)
            lane = 48 * head
            lse = stats[:, lane : lane + 1] + stats[:, lane + 16 : lane + 17] + stats[:, lane + 32 : lane + 33]
            lse = jnp.where(known, wide(lse, CHIPS * WHOLE).reshape(CHIPS, WHOLE, HD), NEG)
            top = jnp.max(lse, axis=0)
            weight = jnp.exp2(lse - top[None])
            total = jnp.sum(weight, axis=0)
            merged.append((jnp.sum(weight * parts, axis=0) / total, top + jnp.log2(total)))
        return merged

    def last_merge(head, whole):
        c = cols(head)
        group = (out1[head], lse1[head])
        rows = pl.ds(offs1[head], SEL, stride=GROUP)
        small[0:SEL, c] = merge([(out0[head, rows, :], lse0[head, rows, :]), group])[0]
        rows = pl.ds(offs2[head], WHOLE, stride=GROUP * GROUPS)
        rows1 = pl.ds(offs2[head] // GROUP, WHOLE, stride=GROUPS)
        same = jnp.full((WHOLE, HD), offs2[head] % GROUP) == offs1[head]
        lse = jnp.where(same, lse1[head, rows1, :], NEG)
        parts = [(out0[head, rows, :], lse0[head, rows, :]), (out1[head, rows1, :], lse), whole[head]]
        small[SEL : SEL + WHOLE, c] = merge(parts)[0]

    local(7)
    local(6)
    ask(1)
    pair_copies[1][0].start()
    pair_copies[1][1].start()
    local(5)
    each_key(lambda peer: key_copy(peer, peer).wait_recv())
    core_copy.start()
    pair_wait(0)
    group_own(0)
    group_foreign(0)
    core_in.wait_recv()
    each_later(lambda peer: query_copy(peer, peer).wait_recv())
    whole_all()
    each_later(lambda peer: result_copy(peer, chip).start())
    local(4)
    local(3)
    pair_wait(1)
    group_foreign(1)
    group_own(1)
    local(2)
    local(1)
    local(0)
    whole = whole_merge()
    for head in range(HEADS):
        group_merge(head)
        last_merge(head, whole)
    last = pltpu.make_async_copy(small, small_hbm, store.at[BLOCKS])
    last.start()

    each_key(lambda peer: key_copy(peer, inner).wait_send())
    each_earlier(lambda peer: query_copy(peer, chip).wait_send())
    each_later(lambda peer: result_copy(peer, chip).wait_send())
    for block in range(BLOCKS):
        stored(block).wait()
    last.wait()
    core_copy.wait_send()
    for head in range(HEADS):
        for copy in pair_copies[head]:
            copy.wait_send()
        for flow, (_, asks, serves) in enumerate(flows):

            @pl.when(asks)
            def _():
                query_copies[head][flow].wait_send()

            @pl.when(serves)
            def _():
                result_copies[head][flow].wait_send()


SMALL = (SEL + WHOLE + 8, HEADS * HD)


def attention(queries, keys, values, offsets_group, offsets_global):
    hbm = pl.BlockSpec(memory_space=pltpu.HBM)
    dma = pltpu.SemaphoreType.DMA
    width = HEADS * HD
    return pl.pallas_call(
        attention_kernel,
        out_shape=[
            jax.ShapeDtypeStruct((ROWS, width), BF16),
            jax.ShapeDtypeStruct(SMALL, F32),
        ],
        in_specs=[hbm] * 5,
        out_specs=[hbm] * 2,
        scratch_shapes=[
            pltpu.SMEM((HEADS, GROUPS), jnp.int32),
            pltpu.SMEM((HEADS,), jnp.int32),
            pltpu.VMEM((ROWS, width), BF16),
            pltpu.VMEM((ROWS, width), BF16),
            pltpu.VMEM((ROWS, width), BF16),
            pltpu.VMEM((ROWS, 2 * width), BF16),
            pltpu.VMEM((ROWS, width), BF16),
            pltpu.VMEM(SMALL, F32),
            pltpu.VMEM((HEADS, ROWS, HD), F32),
            pltpu.VMEM((HEADS, ROWS, HD), F32),
            pltpu.VMEM((HEADS, SEL, HD), F32),
            pltpu.VMEM((HEADS, SEL, HD), F32),
            pltpu.VMEM((HEADS, 2 * SEL, HD), BF16),
            pltpu.VMEM((HEADS, 2 * SEL, HD), BF16),
            pltpu.VMEM((HEADS, SEL, HD), BF16),
            pltpu.VMEM((HEADS, 3 * SEL, HD), BF16),
            pltpu.VMEM((HEADS, 3, SEL + 16, HD), BF16),
            pltpu.VMEM((HEADS, 3, SEL + 16, HD), BF16),
            pltpu.VMEM((CORES, GROUP * WHOLE, 2 * width), BF16),
            pltpu.VMEM((CHIPS * WHOLE, width), BF16),
            pltpu.VMEM((CHIPS * WHOLE, width + HD), BF16),
            pltpu.VMEM((CHIPS * WHOLE, width + HD), BF16),
            dma((5,)),
            dma((BLOCKS + 1,)),
            dma((17,)),
            dma((17,)),
            dma((GROUP,)),
            dma((GROUP,)),
            dma((CHIPS,)),
            dma((CHIPS,)),
            dma((CHIPS,)),
            dma((CHIPS,)),
        ],
        compiler_params=pltpu.CompilerParams(
            collective_id=0, has_side_effects=True, vmem_limit_bytes=56 * 2**20
        ),
        cost_estimate=pl.CostEstimate(flops=5 * 10**9, bytes_accessed=4 * 2**20, transcendentals=6 * 10**6),
        name="attention",
    )(offsets_group.T, offsets_global, queries, keys, values)


SLOTS = 4


def project_kernel(att_hbm, small_hbm, w_hbm, o_ref, att, small, w_ref, buf, load, sem):
    def copy(block):
        return pltpu.make_async_copy(
            buf.at[block % SLOTS], o_ref.at[pl.ds(block * BQ, BQ)], sem.at[block % SLOTS]
        )

    def load_block(block):
        rows = pl.ds(block * BQ, BQ)
        return pltpu.make_async_copy(att_hbm.at[rows], att.at[rows], load.at[2 + block])

    width = HEADS * HD
    halves = [slice(part * w_ref.shape[1] // 2, (part + 1) * w_ref.shape[1] // 2) for part in range(2)]
    w_copies = [
        pltpu.make_async_copy(w_hbm.at[:, half], w_ref.at[:, half], load.at[1 + BLOCKS * part + part])
        for part, half in enumerate(halves)
    ]
    small_copy = pltpu.make_async_copy(small_hbm, small, load.at[0])
    small_copy.start()
    load_block(0).start()
    for item in w_copies:
        item.start()
    for block in range(1, BLOCKS):
        load_block(block).start()
    small_copy.wait()

    n1 = BQ // GROUP
    n2 = BQ // (GROUP * GROUPS)
    spots = iota((BQ, width), 0)
    low = SEL + WHOLE
    left = iota((1, width), 1) < HD
    offset1 = jnp.where(left, small[low : low + 1, :], small[low + 1 : low + 2, :]).astype(jnp.int32)
    offset2 = jnp.where(left, small[low + 2 : low + 3, :], small[low + 3 : low + 4, :]).astype(jnp.int32)

    def spread(first, count):
        part = small[first : first + count, :]
        return jnp.broadcast_to(part[:, None, :], (count, BQ // count, width)).reshape(BQ, width)

    for block in range(BLOCKS):
        rows = slice(block * BQ, (block + 1) * BQ)
        load_block(block).wait()
        merged = jnp.where(spots % GROUP == offset1, spread(block * n1, n1), att[rows, :].astype(F32))
        merged = jnp.where(spots % (GROUP * GROUPS) == offset2, spread(SEL + block * n2, n2), merged).astype(BF16)
        if block == 0:
            for item, half in zip(w_copies, halves):
                item.wait()
                buf[0, :, half] = dot(merged, w_ref[:, half]).astype(BF16)
        else:
            if block >= SLOTS:
                copy(block - SLOTS).wait()
            buf[block % SLOTS] = dot(merged, w_ref[...]).astype(BF16)
        copy(block).start()
    for block in range(BLOCKS - SLOTS, BLOCKS):
        copy(block).wait()


def project(parts, weight):
    hbm = pl.BlockSpec(memory_space=pltpu.HBM)
    width = weight.shape[1]
    return pl.pallas_call(
        project_kernel,
        out_shape=jax.ShapeDtypeStruct((ROWS, width), BF16),
        in_specs=[hbm] * 3,
        out_specs=hbm,
        scratch_shapes=[
            pltpu.VMEM((ROWS, HEADS * HD), BF16),
            pltpu.VMEM(SMALL, F32),
            pltpu.VMEM((HEADS * HD, width), BF16),
            pltpu.VMEM((SLOTS, BQ, width), BF16),
            pltpu.SemaphoreType.DMA((3 + BLOCKS,)),
            pltpu.SemaphoreType.DMA((SLOTS,)),
        ],
        compiler_params=pltpu.CompilerParams(vmem_limit_bytes=56 * 2**20),
        cost_estimate=pl.CostEstimate(flops=43 * 10**8, bytes_accessed=19 * 2**20, transcendentals=0),
        name="project",
    )(*parts, weight)


def per_device(queries, keys, values, offsets_group, offsets_global, out_weight):
    return project(attention(queries, keys, values, offsets_group, offsets_global), out_weight)


def solution(mesh):
    rows = P(("outer", "inner"), None)
    return jax.shard_map(
        per_device, mesh=mesh, in_specs=(rows, rows, rows, P(), P(), P()), out_specs=rows, check_vma=False
    )
```

```python
import functools

import jax
import jax.numpy as jnp
from jax import lax
from jax.experimental import pallas as pl
from jax.experimental.pallas import tpu as pltpu
from jax.sharding import PartitionSpec as P

HD = 128
HEADS = 2
ROWS = 2048
RING = 4
PLANES = 2
GROUP = RING * PLANES
GROUPS = 16
CORES = 2
CHIPS = GROUPS // CORES
SEL = ROWS // GROUP
WHOLE = ROWS // (GROUP * GROUPS)
BQ = 256
BLOCKS = ROWS // BQ
SCALE = HD**-0.5 * 1.4426950408889634
NEG = -1e30
F32 = jnp.float32
BF16 = jnp.bfloat16


def iota(shape, dim):
    return lax.broadcasted_iota(jnp.int32, shape, dim)


def cols(head):
    return slice(head * HD, (head + 1) * HD)


def dot_t(a, b):
    return lax.dot_general(a, b, (((1,), (1,)), ((), ())), preferred_element_type=F32)


def dot(a, b):
    return jnp.dot(a, b, preferred_element_type=F32)


def wide(column, rows):
    return jnp.broadcast_to(column, (rows, HD))


def finish(scores, values):
    rows = scores.shape[0]
    top = jnp.max(scores, axis=1, keepdims=True)
    expo = jnp.exp2((scores - top) * SCALE)
    total = jnp.sum(expo, axis=1, keepdims=True)
    out = dot(expo.astype(BF16), values) / total
    return out, wide(top * SCALE + jnp.log2(total), rows)


def local_tile(q_ref, k_ref, vx_ref, block, head):
    low = block * BQ
    high = low + BQ
    scores = dot_t(q_ref[low:high, cols(head)], k_ref[0:high, cols(head)])
    diag = jnp.where(iota((BQ, BQ), 1) <= iota((BQ, BQ), 0), scores[:, low:], NEG)
    scores = diag if block == 0 else jnp.concatenate([scores[:, :low], diag], axis=1)
    top = jnp.max(scores, axis=1, keepdims=True)
    expo = jnp.exp2((scores - top) * SCALE)
    out = dot(expo.astype(BF16), vx_ref[0:high, head * 2 * HD : (head + 1) * 2 * HD])
    total = out[:, HD:]
    return out[:, :HD] / total, top * SCALE + jnp.log2(total)


def merge(parts):
    top = parts[0][1]
    for _, lse in parts[1:]:
        top = jnp.maximum(top, lse)
    weights = [jnp.exp2(lse - top) for _, lse in parts]
    out = sum(weight * part for weight, (part, _) in zip(weights, parts))
    total = sum(weights)
    return out / total, top + jnp.log2(total)


def three_terms(value, place):
    result = jnp.zeros(value.shape, F32)
    for term in range(3):
        head = value.astype(BF16).astype(F32)
        value = value - head
        result = jnp.where(place == term, head, result)
    return result.astype(BF16)


def pack_lse(lse):
    flat = lse.T[0:16, :]
    row = iota((16, HD), 0)
    return three_terms(jnp.where(row % 2 == 0, flat[:, :HD], flat[:, HD:]), row // 2)


def unpack_lse(packed):
    rows = packed.astype(F32)
    halves = [rows[h : h + 1] + rows[h + 2 : h + 3] + rows[h + 4 : h + 5] for h in range(2)]
    flat = jnp.concatenate(halves, axis=1)
    return jnp.broadcast_to(flat, (HD, SEL)).T


def attention_kernel(
    offg_hbm, offw_hbm, q_hbm, k_hbm, v_hbm,
    att_hbm, small_hbm,
    offg_ref, offw_ref, q_ref, k_ref, v_ref, vx, att, small, out0, lse0, out1, lse1,
    gk, gv, gq, gqr, gos, gor,
    nkv, nq, no_out, no_in,
    load, store, send, recv, wk_send, wk_recv, wq_send, wq_recv, wo_send, wo_recv,
):
    outer = lax.axis_index("outer")
    inner = lax.axis_index("inner")
    plane = inner // RING
    y = inner % RING
    chip = outer // CORES
    core = outer % CORES
    base = plane * RING
    pair = base + (y // 2) * 2 + 1 - y % 2
    across = (1 - plane) * RING + y
    reverse = base + RING - 1 - y
    diagonal = (1 - plane) * RING + RING - 1 - y
    other_core = chip * CORES + 1 - core
    mesh_id = pl.DeviceIdType.MESH

    barrier = pltpu.get_barrier_semaphore()

    def greet_inner(step, carry):
        pl.semaphore_signal(barrier, inc=1, device_id={"inner": (inner + step) % GROUP}, device_id_type=mesh_id)
        return carry

    def greet_outer(peer, carry):
        pl.semaphore_signal(barrier, inc=1, device_id={"outer": peer * CORES + core}, device_id_type=mesh_id)
        return carry

    lax.fori_loop(1, GROUP, greet_inner, 0)
    lax.fori_loop(chip + 1, CHIPS, greet_outer, 0)
    pl.semaphore_signal(barrier, inc=1, device_id={"outer": other_core}, device_id_type=mesh_id)

    loads = [
        pltpu.make_async_copy(src, dst, load.at[index])
        for index, (src, dst) in enumerate(
            ((offg_hbm, offg_ref), (offw_hbm, offw_ref), (k_hbm, k_ref), (v_hbm, v_ref), (q_hbm, q_ref))
        )
    ]
    for copy in loads:
        copy.start()
    loads[0].wait()
    loads[1].wait()

    offs1 = [offg_ref[head, outer] for head in range(HEADS)]
    offs2 = [offw_ref[head] for head in range(HEADS)]
    row8 = iota((8, HD), 0)
    offsets = jnp.where(
        row8 == 0, offs1[0], jnp.where(row8 == 1, offs1[1], jnp.where(row8 == 2, offs2[0], offs2[1]))
    )
    for head in range(HEADS):
        small[SEL + WHOLE : SEL + WHOLE + 8, cols(head)] = offsets.astype(F32)
    n1 = BQ // GROUP
    pick1 = [
        (iota((n1, BQ), 1) == iota((n1, BQ), 0) * GROUP + offs1[head]).astype(F32).astype(BF16)
        for head in range(HEADS)
    ]
    picks = []
    for block in range(BLOCKS):
        pick2 = [
            (iota((WHOLE, BQ), 1) + block * BQ == iota((WHOLE, BQ), 0) * (GROUP * GROUPS) + offs2[head])
            .astype(F32).astype(BF16)
            for head in range(HEADS)
        ]
        picks.append(jnp.concatenate(pick1 + pick2, axis=0))
    own1 = pl.multiple_of((y % 2) * SEL, SEL)
    own2 = pl.multiple_of(inner * WHOLE, WHOLE)
    own3 = pl.multiple_of(chip * WHOLE, WHOLE)
    def select(index):
        ref = (k_ref, v_ref, q_ref)[index]
        loads[2 + index].wait()
        whole = [jnp.zeros((WHOLE, HD), F32) for _ in range(HEADS)]
        for block in range(BLOCKS):
            got = dot(picks[block], ref[block * BQ : (block + 1) * BQ, :])
            for head in range(HEADS):
                rows1 = got[head * n1 : (head + 1) * n1, cols(head)].astype(BF16)
                if index == 2:
                    gq[head, block * n1 : (block + 1) * n1, :] = rows1
                else:
                    (gk, gv)[index][head, pl.ds(own1 + block * n1, n1), :] = rows1
                low = HEADS * n1 + head * WHOLE
                whole[head] += got[low : low + WHOLE, cols(head)]
        for head in range(HEADS):
            if index == 2:
                nq[pl.ds(own3, WHOLE), cols(head)] = whole[head].astype(BF16)
            else:
                nkv[core, pl.ds(own2, WHOLE), cols(index * HEADS + head)] = whole[head].astype(BF16)

    def remote(src, dst, index, axis, peer):
        return pltpu.make_async_remote_copy(
            src_ref=src, dst_ref=dst, send_sem=send.at[index], recv_sem=recv.at[index],
            device_id={axis: peer}, device_id_type=mesh_id,
        )

    def slot(index):
        return pl.ds(pl.multiple_of(index * WHOLE, WHOLE), WHOLE)

    def key_copy(peer, index):
        return pltpu.make_async_remote_copy(
            src_ref=nkv.at[core, slot(inner)], dst_ref=nkv.at[core, slot(index)],
            send_sem=wk_send.at[peer], recv_sem=wk_recv.at[index],
            device_id={"inner": peer}, device_id_type=mesh_id,
        )

    def query_copy(peer, index):
        return pltpu.make_async_remote_copy(
            src_ref=nq.at[slot(chip)], dst_ref=nq.at[slot(index)],
            send_sem=wq_send.at[peer], recv_sem=wq_recv.at[index],
            device_id={"outer": peer * CORES + core}, device_id_type=mesh_id,
        )

    def result_copy(peer, index):
        return pltpu.make_async_remote_copy(
            src_ref=no_out.at[slot(peer)], dst_ref=no_in.at[slot(index)],
            send_sem=wo_send.at[peer], recv_sem=wo_recv.at[index],
            device_id={"outer": peer * CORES + core}, device_id_type=mesh_id,
        )

    core_copy = remote(nkv.at[core], nkv.at[core], 0, "outer", other_core)
    core_in = remote(nkv.at[1 - core], nkv.at[1 - core], 0, "outer", other_core)

    def each(first, last, act):
        def body(index, carry):
            act(index)
            return carry

        lax.fori_loop(first, last, body, 0)

    def each_key(act):
        each(1, GROUP, lambda step: act((inner + step) % GROUP))

    def each_earlier(act):
        each(0, chip, act)

    def each_later(act):
        each(chip + 1, CHIPS, act)

    flows = (
        (across, plane == 1, plane == 0),
        (diagonal, plane == 1, plane == 0),
        (reverse, y >= 2, y < 2),
    )
    pair_copies = []
    query_copies = []
    result_copies = []
    for head in range(HEADS):
        place = 1 + head * 8
        rows = pl.ds(own1, SEL)
        pair_copies.append(
            [
                remote(buffer.at[head, rows], buffer.at[head, rows], place + index, "inner", pair)
                for index, buffer in enumerate((gk, gv))
            ]
        )
        query_copies.append(
            [
                remote(gq.at[head], gqr.at[head, pl.ds(flow * SEL, SEL)], place + 2 + flow, "inner", peer)
                for flow, (peer, _, _) in enumerate(flows)
            ]
        )
        result_copies.append(
            [
                remote(gos.at[head, flow], gor.at[head, flow], place + 5 + flow, "inner", peer)
                for flow, (peer, _, _) in enumerate(flows)
            ]
        )

    def ask(head):
        @pl.when(plane == 1)
        def _():
            query_copies[head][1].start()
            query_copies[head][0].start()

        @pl.when(y >= 2)
        def _():
            query_copies[head][2].start()

    select(0)
    select(1)
    pl.semaphore_wait(barrier, GROUP - 1 + 1 + chip)
    each_key(lambda peer: key_copy(peer, inner).start())
    pair_copies[0][0].start()
    pair_copies[0][1].start()
    select(2)
    ask(0)
    each_earlier(lambda peer: query_copy(peer, chip).start())

    for head in range(HEADS):
        vx[:, 2 * head * HD : (2 * head + 1) * HD] = v_ref[:, cols(head)]
        vx[:, (2 * head + 1) * HD : (2 * head + 2) * HD] = jnp.ones((ROWS, HD), BF16)

    def stored(block):
        rows = pl.ds(block * BQ, BQ)
        return pltpu.make_async_copy(att.at[rows], att_hbm.at[rows], store.at[block])

    def local(block):
        for head in range(HEADS):
            c = cols(head)
            out, lse = local_tile(q_ref, k_ref, vx, block, head)
            att[block * BQ : (block + 1) * BQ, c] = out.astype(BF16)
            out0[head, block * BQ : (block + 1) * BQ, :] = out
            lse0[head, block * BQ : (block + 1) * BQ, :] = lse
        stored(block).start()

    def group_foreign(head):
        def serve(first, count):
            for flow in range(first, first + count):
                query_copies[head][flow].wait_recv()
            out, lse = finish(dot_t(gqr[head, first * SEL : (first + count) * SEL, :], gk[head]), gv[head])
            for index in range(count):
                rows = slice(index * SEL, (index + 1) * SEL)
                gos[head, first + index, 0:SEL, :] = out[rows].astype(BF16)
                gos[head, first + index, SEL : SEL + 16, :] = pack_lse(lse[rows])
                result_copies[head][first + index].start()

        @pl.when(plane == 0)
        def _():
            serve(1, 1)
            serve(0, 1)

        @pl.when(y < 2)
        def _():
            serve(2, 1)

    def pair_wait(head):
        for copy in pair_copies[head]:
            copy.wait_recv()

    def group_own(head):
        scores = dot_t(gq[head], gk[head])
        shape = (SEL, 2 * SEL)
        out, lse = finish(jnp.where(iota(shape, 1) <= iota(shape, 0) + own1, scores, NEG), gv[head])
        out1[head] = out
        lse1[head] = lse

    def group_merge(head):
        c = cols(head)
        for flow, (_, asks, _) in enumerate(flows):

            @pl.when(asks)
            def _():
                result_copies[head][flow].wait_recv()
                here = (out1[head], lse1[head])
                there = (gor[head, flow, 0:SEL, :].astype(F32), unpack_lse(gor[head, flow, SEL : SEL + 16, :]))
                out1[head], lse1[head] = merge([here, there])

    def whole_all():
        rows = CHIPS * WHOLE
        keys = CORES * GROUP * WHOLE
        shape = (rows, keys)
        row = iota(shape, 0)
        query_pos = (row // WHOLE * CORES + core) * GROUP * WHOLE + inner * WHOLE + row % WHOLE
        allowed = iota(shape, 1) + chip * keys <= query_pos
        place = iota((rows, HD), 1) // 16
        stats = jnp.zeros((rows, HD), F32)
        for head in range(HEADS):
            key_rows = nkv[:, :, cols(head)].reshape(keys, HD)
            value_rows = nkv[:, :, cols(HEADS + head)].reshape(keys, HD)
            out, lse = finish(jnp.where(allowed, dot_t(nq[:, cols(head)], key_rows), NEG), value_rows)
            no_out[:, cols(head)] = out.astype(BF16)
            stats = stats + three_terms(lse, place - 3 * head).astype(F32)
        no_out[:, cols(HEADS)] = stats.astype(BF16)
        no_in[slot(chip), :] = no_out[slot(chip), :]

    def whole_merge():
        each_earlier(lambda peer: result_copy(peer, peer).wait_recv())
        stats = no_in[:, cols(HEADS)].astype(F32)
        known = iota((CHIPS, WHOLE, HD), 0) <= chip
        merged = []
        for head in range(HEADS):
            parts = jnp.where(known, no_in[:, cols(head)].astype(F32).reshape(CHIPS, WHOLE, HD), 0.0)
            lane = 48 * head
            lse = stats[:, lane : lane + 1] + stats[:, lane + 16 : lane + 17] + stats[:, lane + 32 : lane + 33]
            lse = jnp.where(known, wide(lse, CHIPS * WHOLE).reshape(CHIPS, WHOLE, HD), NEG)
            top = jnp.max(lse, axis=0)
            weight = jnp.exp2(lse - top[None])
            total = jnp.sum(weight, axis=0)
            merged.append((jnp.sum(weight * parts, axis=0) / total, top + jnp.log2(total)))
        return merged

    def last_merge(head, whole):
        c = cols(head)
        group = (out1[head], lse1[head])
        rows = pl.ds(offs1[head], SEL, stride=GROUP)
        small[0:SEL, c] = merge([(out0[head, rows, :], lse0[head, rows, :]), group])[0]
        rows = pl.ds(offs2[head], WHOLE, stride=GROUP * GROUPS)
        rows1 = pl.ds(offs2[head] // GROUP, WHOLE, stride=GROUPS)
        same = jnp.full((WHOLE, HD), offs2[head] % GROUP) == offs1[head]
        lse = jnp.where(same, lse1[head, rows1, :], NEG)
        parts = [(out0[head, rows, :], lse0[head, rows, :]), (out1[head, rows1, :], lse), whole[head]]
        small[SEL : SEL + WHOLE, c] = merge(parts)[0]

    local(7)
    local(6)
    ask(1)
    pair_copies[1][0].start()
    pair_copies[1][1].start()
    local(5)
    each_key(lambda peer: key_copy(peer, peer).wait_recv())
    core_copy.start()
    pair_wait(0)
    group_own(0)
    group_foreign(0)
    core_in.wait_recv()
    each_later(lambda peer: query_copy(peer, peer).wait_recv())
    whole_all()
    each_later(lambda peer: result_copy(peer, chip).start())
    local(4)
    pair_wait(1)
    group_foreign(1)
    local(3)
    group_own(1)
    local(2)
    local(1)
    local(0)
    whole = whole_merge()
    for head in range(HEADS):
        group_merge(head)
        last_merge(head, whole)
    last = pltpu.make_async_copy(small, small_hbm, store.at[BLOCKS])
    last.start()

    each_key(lambda peer: key_copy(peer, inner).wait_send())
    each_earlier(lambda peer: query_copy(peer, chip).wait_send())
    each_later(lambda peer: result_copy(peer, chip).wait_send())
    for block in range(BLOCKS):
        stored(block).wait()
    last.wait()
    core_copy.wait_send()
    for head in range(HEADS):
        for copy in pair_copies[head]:
            copy.wait_send()
        for flow, (_, asks, serves) in enumerate(flows):

            @pl.when(asks)
            def _():
                query_copies[head][flow].wait_send()

            @pl.when(serves)
            def _():
                result_copies[head][flow].wait_send()


SMALL = (SEL + WHOLE + 8, HEADS * HD)


def attention(queries, keys, values, offsets_group, offsets_global):
    hbm = pl.BlockSpec(memory_space=pltpu.HBM)
    dma = pltpu.SemaphoreType.DMA
    width = HEADS * HD
    return pl.pallas_call(
        attention_kernel,
        out_shape=[
            jax.ShapeDtypeStruct((ROWS, width), BF16),
            jax.ShapeDtypeStruct(SMALL, F32),
        ],
        in_specs=[hbm] * 5,
        out_specs=[hbm] * 2,
        scratch_shapes=[
            pltpu.SMEM((HEADS, GROUPS), jnp.int32),
            pltpu.SMEM((HEADS,), jnp.int32),
            pltpu.VMEM((ROWS, width), BF16),
            pltpu.VMEM((ROWS, width), BF16),
            pltpu.VMEM((ROWS, width), BF16),
            pltpu.VMEM((ROWS, 2 * width), BF16),
            pltpu.VMEM((ROWS, width), BF16),
            pltpu.VMEM(SMALL, F32),
            pltpu.VMEM((HEADS, ROWS, HD), F32),
            pltpu.VMEM((HEADS, ROWS, HD), F32),
            pltpu.VMEM((HEADS, SEL, HD), F32),
            pltpu.VMEM((HEADS, SEL, HD), F32),
            pltpu.VMEM((HEADS, 2 * SEL, HD), BF16),
            pltpu.VMEM((HEADS, 2 * SEL, HD), BF16),
            pltpu.VMEM((HEADS, SEL, HD), BF16),
            pltpu.VMEM((HEADS, 3 * SEL, HD), BF16),
            pltpu.VMEM((HEADS, 3, SEL + 16, HD), BF16),
            pltpu.VMEM((HEADS, 3, SEL + 16, HD), BF16),
            pltpu.VMEM((CORES, GROUP * WHOLE, 2 * width), BF16),
            pltpu.VMEM((CHIPS * WHOLE, width), BF16),
            pltpu.VMEM((CHIPS * WHOLE, width + HD), BF16),
            pltpu.VMEM((CHIPS * WHOLE, width + HD), BF16),
            dma((5,)),
            dma((BLOCKS + 1,)),
            dma((17,)),
            dma((17,)),
            dma((GROUP,)),
            dma((GROUP,)),
            dma((CHIPS,)),
            dma((CHIPS,)),
            dma((CHIPS,)),
            dma((CHIPS,)),
        ],
        compiler_params=pltpu.CompilerParams(
            collective_id=0, has_side_effects=True, vmem_limit_bytes=56 * 2**20
        ),
        cost_estimate=pl.CostEstimate(flops=5 * 10**9, bytes_accessed=4 * 2**20, transcendentals=6 * 10**6),
        name="attention",
    )(offsets_group.T, offsets_global, queries, keys, values)


SLOTS = 4


def project_kernel(att_hbm, small_hbm, w_hbm, o_ref, att, small, w_ref, buf, load, sem):
    def copy(block):
        return pltpu.make_async_copy(
            buf.at[block % SLOTS], o_ref.at[pl.ds(block * BQ, BQ)], sem.at[block % SLOTS]
        )

    def load_block(block):
        rows = pl.ds(block * BQ, BQ)
        return pltpu.make_async_copy(att_hbm.at[rows], att.at[rows], load.at[2 + block])

    width = HEADS * HD
    halves = [slice(part * w_ref.shape[1] // 2, (part + 1) * w_ref.shape[1] // 2) for part in range(2)]
    w_copies = [
        pltpu.make_async_copy(w_hbm.at[:, half], w_ref.at[:, half], load.at[1 + BLOCKS * part + part])
        for part, half in enumerate(halves)
    ]
    small_copy = pltpu.make_async_copy(small_hbm, small, load.at[0])
    small_copy.start()
    load_block(0).start()
    for item in w_copies:
        item.start()
    for block in range(1, BLOCKS):
        load_block(block).start()
    small_copy.wait()

    n1 = BQ // GROUP
    n2 = BQ // (GROUP * GROUPS)
    spots = iota((BQ, width), 0)
    low = SEL + WHOLE
    left = iota((1, width), 1) < HD
    offset1 = jnp.where(left, small[low : low + 1, :], small[low + 1 : low + 2, :]).astype(jnp.int32)
    offset2 = jnp.where(left, small[low + 2 : low + 3, :], small[low + 3 : low + 4, :]).astype(jnp.int32)

    def spread(first, count):
        part = small[first : first + count, :]
        return jnp.broadcast_to(part[:, None, :], (count, BQ // count, width)).reshape(BQ, width)

    for block in range(BLOCKS):
        rows = slice(block * BQ, (block + 1) * BQ)
        load_block(block).wait()
        merged = jnp.where(spots % GROUP == offset1, spread(block * n1, n1), att[rows, :].astype(F32))
        merged = jnp.where(spots % (GROUP * GROUPS) == offset2, spread(SEL + block * n2, n2), merged).astype(BF16)
        if block == 0:
            for item, half in zip(w_copies, halves):
                item.wait()
                buf[0, :, half] = dot(merged, w_ref[:, half]).astype(BF16)
        else:
            if block >= SLOTS:
                copy(block - SLOTS).wait()
            buf[block % SLOTS] = dot(merged, w_ref[...]).astype(BF16)
        copy(block).start()
    for block in range(BLOCKS - SLOTS, BLOCKS):
        copy(block).wait()


def project(parts, weight):
    hbm = pl.BlockSpec(memory_space=pltpu.HBM)
    width = weight.shape[1]
    return pl.pallas_call(
        project_kernel,
        out_shape=jax.ShapeDtypeStruct((ROWS, width), BF16),
        in_specs=[hbm] * 3,
        out_specs=hbm,
        scratch_shapes=[
            pltpu.VMEM((ROWS, HEADS * HD), BF16),
            pltpu.VMEM(SMALL, F32),
            pltpu.VMEM((HEADS * HD, width), BF16),
            pltpu.VMEM((SLOTS, BQ, width), BF16),
            pltpu.SemaphoreType.DMA((3 + BLOCKS,)),
            pltpu.SemaphoreType.DMA((SLOTS,)),
        ],
        compiler_params=pltpu.CompilerParams(vmem_limit_bytes=56 * 2**20),
        cost_estimate=pl.CostEstimate(flops=43 * 10**8, bytes_accessed=19 * 2**20, transcendentals=0),
        name="project",
    )(*parts, weight)


def per_device(queries, keys, values, offsets_group, offsets_global, out_weight):
    return project(attention(queries, keys, values, offsets_group, offsets_global), out_weight)


def solution(mesh):
    rows = P(("outer", "inner"), None)
    return jax.shard_map(
        per_device, mesh=mesh, in_specs=(rows, rows, rows, P(), P(), P()), out_specs=rows, check_vma=False
    )
```
